256 devices in a mesh: vocab: 32 (over y, z_lo, core), rep: 8 (over x, z_hi).
Axes of the slice: x: 4, y: 4, z: 8 (z_hi: 2, z_lo: 4; z = z_hi * 4 + z_lo), core: 2. Of those that a mesh axis runs over, the one named last changes fastest.
Arguments:
- src_ids: int32 [8, 256], P('rep'), may hold values from 0 to 131071
- tgt_ids: int32 [8, 128], P('rep'), may hold values from 0 to 131071
- tgt_mask: int32 [8, 128], P('rep'), may hold values from 0 to 1, as said below
- tgt_order: int32 [8, 128], P('rep'), may hold values from 0 to 127, each once within a row
- table: bfloat16 [131072, 1024], P('vocab'), may hold values from -0.6 to 0.6
- student_hidden: bfloat16 [8, 128, 1024], P('rep'), may hold values from -30 to 30
- teacher_hidden: bfloat16 [8, 128, 2048], P('rep', 'vocab'), may hold values from -25 to 25
- teacher_head: bfloat16 [131072, 2048], P('vocab', 'rep'), may hold values from -0.45 to 0.45
- src_embed_grad: bfloat16 [8, 256, 1024], P('rep'), may hold values from -0.4375 to 0.4375
- tgt_embed_grad: bfloat16 [8, 128, 1024], P('rep'), may hold values from -0.4375 to 0.4375
Outputs:
- src_embeds: bfloat16 [8, 256, 1024], P('rep', 'vocab')
- tgt_embeds: bfloat16 [8, 128, 1024], P('rep', 'vocab')
- kl_loss: float32 [], replicated
- hidden_grad: float32 [8, 128, 1024], P('rep', 'vocab')
- table_grad: bfloat16 [131072, 1024], P(('vocab', 'rep'))
The draws below stay inside these ranges and needn't reach their ends.
Inputs may be any that keep to these rules, and one draw needn't show every extreme that they name: `tgt_mask`: each replica's mask is 1 on a prefix of at least 32 positions and 0 after it; in every draw one replica's mask is all ones. Row r lists every position of 0 to 127 once; teacher_hidden[r, j] is the teacher state of target position tgt_order[r, j].
All inputs are finite; a program needn't handle non-finite values.
Results may differ from the reference program's by a relative error of at most 0.0031.
Values may be sent and summed in bfloat16 or wider, within the bound.
A program may use at most 128 MiB of HBM per device.

```python
import math
import jax
import jax.numpy as jnp
import numpy as np
from jax import lax

D = 1024
DT = 2048
TGT = 128
SRC = 256
VOCAB = 131072
REPS = 8


gain_levels = (15.0, 25.0, 35.0, 45.0)


def pick_pairs(key, salt, total_rows, vocab_rows):
    pair_key = jax.random.fold_in(key, salt)
    first_key, second_key = jax.random.split(pair_key)
    positions = jax.random.permutation(first_key, total_rows)[:4]
    sources = jax.random.randint(second_key, (4,), 0, vocab_rows // 2)
    return (positions, sources, sources + vocab_rows // 2)


def base_matrix(key, salt, shape, spread):
    values = jax.random.normal(jax.random.fold_in(key, salt), shape, jnp.float32)
    return jnp.clip(values, -6.0, 6.0) * spread


def draw_table(key, part):
    base = base_matrix(key, 11, (VOCAB, D), 0.1)
    positions, sources, targets = pick_pairs(key, 21, REPS * TGT, VOCAB)
    factors = 1.0 - 2.0 / (jnp.array(gain_levels, jnp.float32) * 0.01 * D)
    base = base.at[targets].set(base[sources] * factors[:, None])
    return base.astype(jnp.bfloat16)


def draw_student_hidden(key, part):
    positions, sources, targets = pick_pairs(key, 21, REPS * TGT, VOCAB)
    table_rows = base_matrix(key, 11, (VOCAB, D), 0.1)[sources]
    key = jax.random.fold_in(key, 2)
    states = jnp.clip(jax.random.normal(key, (REPS * TGT, D), jnp.float32), -6.0, 6.0)
    states = states.at[positions].set(jnp.array(gain_levels, jnp.float32)[:, None] * table_rows)
    return states.reshape(REPS, TGT, D).astype(jnp.bfloat16)


def draw_teacher_head(key, part):
    base = base_matrix(key, 12, (VOCAB, DT), 0.07)
    positions, sources, targets = pick_pairs(key, 22, REPS * TGT, VOCAB)
    factors = 1.0 - 2.0 / (jnp.array(gain_levels, jnp.float32) * 0.0049 * DT)
    base = base.at[targets].set(base[sources] * factors[:, None])
    return base.astype(jnp.bfloat16)


def draw_teacher_hidden(key, part):
    positions, sources, targets = pick_pairs(key, 22, REPS * TGT, VOCAB)
    head_rows = base_matrix(key, 12, (VOCAB, DT), 0.07)[sources]
    key = jax.random.fold_in(key, 4)
    states = jnp.clip(jax.random.normal(key, (REPS * TGT, DT), jnp.float32), -6.0, 6.0)
    states = states.at[positions].set(jnp.array(gain_levels, jnp.float32)[:, None] * head_rows)
    return states.reshape(REPS, TGT, DT).astype(jnp.bfloat16)


def draw_tgt_mask(key, part):
    key = jax.random.fold_in(key, 5)
    length_key, full_key = jax.random.split(key)
    lengths = jax.random.randint(length_key, (REPS,), TGT // 4, TGT + 1)
    full_row = jax.random.randint(full_key, (), 0, REPS)
    lengths = lengths.at[full_row].set(TGT)
    positions = jnp.arange(TGT, dtype=jnp.int32)
    return (positions[None, :] < lengths[:, None]).astype(jnp.int32)


def place_ends(values, key, least, top_value):
    longest = values.shape.index(max(values.shape))
    spots = []
    for shift in (0, 1):
        where = [jax.random.randint(jax.random.fold_in(key, axis), (), 0, length) for axis, length in enumerate(values.shape)]
        where[longest] = (where[longest] + shift) % values.shape[longest]
        spots.append(tuple(where))
    return values.at[spots[0]].set(least).at[spots[1]].set(top_value)


def steps_of(stream_key, dims, cuts, smallest, high):
    level = 1.0
    for position, blocks in cuts:
        heights = jax.random.uniform(jax.random.fold_in(jax.random.fold_in(stream_key, 6), position), (blocks,), jnp.float32, smallest / len(cuts), high / len(cuts))
        level = level * jnp.repeat(jnp.exp(heights), dims[position] // blocks).reshape((-1,) + (1,) * (len(dims) - 1 - position))
    return level


def wide_ids(stream_key, extent, number_of, slope):
    loads = [min(1 << octave, number_of + 1 - (1 << octave)) * (1 << 20) // math.isqrt((1 << octave) ** slope) + 1 for octave in range((number_of + 1).bit_length()) if 1 << octave <= number_of]
    scale = 1 + sum(loads) // (1 << 30)
    table = np.cumsum(np.array([max(1, weight // scale) for weight in loads]))
    ticket = jax.random.randint(jax.random.fold_in(stream_key, 1), extent, 0, int(table[len(loads) - 1]))
    start = jnp.left_shift(1, jnp.searchsorted(jnp.asarray(table, jnp.int32), ticket, side="right").astype(jnp.int32))
    standing = start - 1 + jax.random.randint(jax.random.fold_in(stream_key, 4), extent, 0, 1 << 30) % jnp.minimum(start, number_of + 1 - start)
    return jax.random.permutation(jax.random.fold_in(stream_key, 2), number_of)[standing].astype(jnp.int32)


def centred(own_key, dims, scale, limit, pieces=(), kind=jnp.bfloat16):
    level = steps_of(own_key, dims, pieces, -0.22, 0.18) if pieces else 1.0
    drawn = jax.random.normal(own_key, dims, jnp.float32) * scale * level
    return jnp.minimum(jnp.maximum(drawn, -limit), limit).astype(kind)


def setup_inputs(seed: int = 0) -> dict:
    arg_keys = jax.random.split(jax.random.key(seed), 11)
    return {
        "src_ids": place_ends(wide_ids(arg_keys[0], (REPS, SRC), VOCAB, 2), jax.random.fold_in(arg_keys[0], 3), 0, VOCAB - 1).astype(jnp.int32),
        "tgt_ids": place_ends(wide_ids(arg_keys[1], (REPS, TGT), VOCAB, 2), jax.random.fold_in(arg_keys[1], 3), 0, VOCAB - 1).astype(jnp.int32),
        "tgt_mask": draw_tgt_mask(jax.random.fold_in(arg_keys[10], 71), 0),
        "tgt_order": jax.vmap(lambda own: jax.random.permutation(own, TGT))(jax.random.split(arg_keys[3], REPS)).reshape((REPS, TGT)).astype(jnp.int32),
        "table": draw_table(jax.random.fold_in(arg_keys[10], 71), 0),
        "student_hidden": draw_student_hidden(jax.random.fold_in(arg_keys[10], 71), 0),
        "teacher_hidden": draw_teacher_hidden(jax.random.fold_in(arg_keys[10], 71), 0),
        "teacher_head": draw_teacher_head(jax.random.fold_in(arg_keys[10], 71), 0),
        "src_embed_grad": centred(arg_keys[8], (REPS, SRC, D), 0.03, 0.4375, ((0, 8),)),
        "tgt_embed_grad": centred(arg_keys[9], (REPS, TGT, D), 0.03, 0.4375, ((0, 8),)),
    }


def contract_last(first, second):
    return lax.dot_general(first, second, (((1,), (1,)), ((), ())), preferred_element_type=jnp.float32)

def contract_first(first, second):
    return lax.dot_general(first, second, (((0,), (0,)), ((), ())), preferred_element_type=jnp.float32)

def place_rows(arrived, order_row):
    return jnp.zeros_like(arrived).at[order_row].set(arrived)

def reference(src_ids, tgt_ids, tgt_mask, tgt_order, table, student_hidden, teacher_hidden, teacher_head, src_embed_grad, tgt_embed_grad):
    embed_scale = math.sqrt(D)
    src_embeds = (table[src_ids].astype(jnp.float32) * embed_scale).astype(jnp.bfloat16)
    tgt_embeds = (table[tgt_ids].astype(jnp.float32) * embed_scale).astype(jnp.bfloat16)
    ordered_states = jax.vmap(place_rows)(teacher_hidden, tgt_order)
    mask_float = tgt_mask.astype(jnp.float32)
    mask_total = jnp.sum(mask_float)
    token_weight = mask_float * (REPS * TGT) / mask_total

    def one_replica(running, inputs):
        hidden, states, weight, mask_row, source_ids, target_ids, source_grad, target_grad = inputs
        student_logits = contract_last(hidden, table)
        teacher_logits = contract_last(states, teacher_head)
        student_top = lax.optimization_barrier(jnp.max(student_logits, axis=1))
        teacher_top = lax.optimization_barrier(jnp.max(teacher_logits, axis=1))
        student_sum = lax.optimization_barrier(jnp.sum(jnp.exp(student_logits - student_top[:, None]), axis=1))
        teacher_exp = jnp.exp(teacher_logits - teacher_top[:, None])
        teacher_sum = lax.optimization_barrier(jnp.sum(teacher_exp, axis=1))
        cross_sum = lax.optimization_barrier(jnp.sum(teacher_exp * (teacher_logits - student_logits), axis=1))
        student_lse = student_top + jnp.log(student_sum)
        teacher_lse = teacher_top + jnp.log(teacher_sum)
        token_kl = cross_sum / teacher_sum - teacher_lse + student_lse
        logit_grad = (weight[:, None] * (jnp.exp(student_logits - student_lse[:, None]) - jnp.exp(teacher_logits - teacher_lse[:, None]))).astype(jnp.bfloat16)
        hidden_grad = jnp.dot(logit_grad, table, preferred_element_type=jnp.float32)
        source_scaled = (source_grad.astype(jnp.float32) * embed_scale).astype(jnp.bfloat16)
        target_scaled = (target_grad.astype(jnp.float32) * embed_scale).astype(jnp.bfloat16)
        lookup_term = jnp.zeros((VOCAB, D), jnp.float32).at[source_ids].add(source_scaled.astype(jnp.float32))
        lookup_term = lookup_term.at[target_ids].add(target_scaled.astype(jnp.float32))
        replica_term = contract_first(logit_grad, hidden) + lookup_term
        return (running + replica_term, (hidden_grad, jnp.sum(mask_row * token_kl)))
    inputs = (student_hidden, ordered_states, token_weight, mask_float, src_ids, tgt_ids, src_embed_grad, tgt_embed_grad)
    grand_total, (hidden_grads, kl_sums) = lax.scan(one_replica, jnp.zeros((VOCAB, D), jnp.float32), inputs)
    kl_loss = jnp.sum(kl_sums) / mask_total
    return (src_embeds, tgt_embeds, kl_loss, hidden_grads, grand_total.astype(jnp.bfloat16))
```

```python
import functools
import math

import jax
import jax.numpy as jnp
from jax import lax
from jax.experimental import pallas as pl
from jax.experimental.pallas import tpu as pltpu
from jax.sharding import PartitionSpec as P

MESH = pl.DeviceIdType.MESH
NX, NY, NZL, NZH, NC = 4, 4, 4, 2, 2
NZ = NZL * NZH
F32, BF16 = jnp.float32, jnp.bfloat16


def dot_nt(a, b):
    return lax.dot_general(a, b, (((1,), (1,)), ((), ())), preferred_element_type=F32)


def dot_nn(a, b):
    return lax.dot_general(a, b, (((1,), (0,)), ((), ())), preferred_element_type=F32)


def dot_tn(a, b):
    return lax.dot_general(a, b, (((0,), (0,)), ((), ())), preferred_element_type=F32)


def merge(own, others):
    groups = own.shape[0] // 4
    tops = [piece[0:4] for piece in [own] + others]
    top = functools.reduce(jnp.maximum, tops)
    total = [0.0] * (groups - 1)
    for piece, piece_top in zip([own] + others, tops):
        factor = jnp.exp(piece_top - top)
        for g in range(1, groups):
            total[g - 1] = total[g - 1] + piece[4 * g : 4 * g + 4] * factor
    return jnp.concatenate([top] + total, axis=0)


def kernel(
    head, table, hidden_in, src_cot, tgt_cot, states_in, meta_in, ids_col,
    emb_out, kl_out, hg_out, tg_out,
    tab, headbuf, hid, cot, st, meta, order_st, slog, tlog, acc, gbuf, gx,
    emb, emb_2, emb_c, emb_y, emb_z,
    sstat, sst_c, sst_x, sst_y, sst_z, tstat, tst_c, tst_x, tst_y, tst_z,
    hp, hp_c, h1, h1_y, h2, h2_z,
    lsem, ssem, rsem,
):
    v, r = lax.axis_index("vocab"), lax.axis_index("rep")
    y, zl, c = v // 8, (v // 2) % 4, v % 2
    x, zh = r // 2, r % 2
    z = zh * 4 + zl
    oc = 1 - c
    oz = 1 - zh

    def dev(y=y, zl=zl, c=c, x=x, zh=zh):
        return ((y * 4 + zl) * 2 + c, x * 2 + zh)

    def zdev(d):
        to = (z + d) % 8
        return dev(zl=to % 4, zh=to // 4)

    used = {"l": 0, "r": 0}
    pending = []

    def local(src, dst):
        i = used["l"]
        used["l"] += 1
        copy = pltpu.make_async_copy(src, dst, lsem.at[i])
        copy.start()
        return copy

    def send(src, dst, to):
        i = used["r"]
        used["r"] += 1
        copy = pltpu.make_async_remote_copy(
            src_ref=src, dst_ref=dst, send_sem=ssem.at[i], recv_sem=rsem.at[i],
            device_id=to, device_id_type=MESH,
        )
        copy.start()
        pending.append(copy)
        return copy

    def arrive(copies):
        for copy in copies:
            copy.wait_recv()

    tab_copies = [local(table.at[pl.ds(b * 512, 512)], tab.at[b]) for b in range(8)]
    st_rows = pl.ds(pl.multiple_of(c * 256 + y * 64 + zl * 16, 16), 16)
    st_rows_y = pl.ds(pl.multiple_of(c * 256 + y * 64, 64), 64)
    st_rows_c = pl.ds(pl.multiple_of(c * 256, 256), 256)
    own_st = local(states_in, st.at[:, x, zh, st_rows, :])
    own_hid = local(hidden_in, hid.at[x, zh])
    own_meta = local(meta_in, meta.at[x, zh])
    own_cot = [
        local(src_cot, cot.at[x, zh, pl.ds(0, 256)]),
        local(tgt_cot, cot.at[x, zh, pl.ds(256, 128)]),
    ]
    own_head = local(head.at[pl.ds(pl.multiple_of(r * 512, 512), 512)], headbuf.at[r])

    own_hid.wait()
    for copy in own_cot:
        copy.wait()

    barrier = pltpu.get_barrier_semaphore()
    rep_offsets = [(dx, dz) for dz in (0, 1) for dx in range(4) if (dx, dz) != (0, 0)]
    peers = [dev(x=(x + dx) % 4, zh=(zh + dz) % 2) for dx, dz in rep_offsets]
    peers += [zdev(d) for d in range(1, 8) if d != 4]
    peers += [dev(y=(y + d) % 4) for d in range(1, 4)]
    peers += [dev(c=oc)]
    for peer in peers:
        pl.semaphore_signal(barrier, inc=1, device_id=peer, device_id_type=MESH)
    pl.semaphore_wait(barrier, len(peers))

    own_st.wait()
    st_z = [
        send(st.at[:, x, zh, st_rows, :], st.at[:, x, zh, st_rows, :], zdev(d)) for d in range(1, 8)
    ]
    own_meta.wait()
    meta_r = [
        send(meta.at[x, zh], meta.at[x, zh], dev(x=(x + dx) % 4, zh=(zh + dz) % 2))
        for dx, dz in rep_offsets
    ]
    hid_8th = pl.ds(pl.multiple_of(c * 64 + y * 16, 16), 16)
    hid_half = pl.ds(pl.multiple_of(c * 64, 64), 64)
    hid_z = [send(hid.at[x, zh, hid_8th], hid.at[x, zh, hid_8th], dev(zh=oz))]
    head_r = []
    for dx, dz in rep_offsets[3:] + rep_offsets[:3]:
        to_x, to_zh = (x + dx) % 4, (zh + dz) % 2
        rows = pl.ds(pl.multiple_of((to_x * 2 + to_zh) * 512, 512), 512)
        head_r.append(send(head.at[rows], headbuf.at[r], dev(x=to_x, zh=to_zh)))
    head_z, head_x = head_r[:4], head_r[4:]
    cot_8th = pl.ds(pl.multiple_of(c * 192 + y * 48, 16), 48)
    cot_half = pl.ds(pl.multiple_of(c * 192, 64), 192)
    cot_z = [send(cot.at[x, zh, cot_8th], cot.at[x, zh, cot_8th], dev(zh=oz))]

    for copy in tab_copies:
        copy.wait()
    lane = lax.broadcasted_iota(jnp.int32, (512, 512), 1)

    def emb_part(b, carry):
        onehot = (ids_col[...] == lane + b * 512).astype(BF16)
        part = dot_nn(onehot, tab[b])

        @pl.when(b == 0)
        def _():
            acc[...] = part

        @pl.when(b != 0)
        def _():
            acc[...] += part

        return carry

    lax.fori_loop(0, 2, emb_part, 0)
    arrive(st_z)
    st_y = [
        send(st.at[:, x, :, st_rows_y, :], st.at[:, x, :, st_rows_y, :], dev(y=(y + d) % 4))
        for d in range(1, 4)
    ]
    arrive(hid_z)
    hid_x = [
        send(hid.at[x, :, hid_8th, :], hid.at[x, :, hid_8th, :], dev(x=(x + d) % 4))
        for d in range(1, 4)
    ]
    lax.fori_loop(2, 4, emb_part, 0)
    arrive(st_y)
    st_x = [
        send(st.at[:, x, :, st_rows_c, :], st.at[:, x, :, st_rows_c, :], dev(x=(x + d) % 4))
        for d in range(1, 4)
    ]
    arrive(hid_x)
    hid_y = [
        send(hid.at[:, :, hid_8th, :], hid.at[:, :, hid_8th, :], dev(y=(y + d) % 4))
        for d in range(1, 4)
    ]
    cot_own_x = [
        send(cot.at[x, zh, cot_half], cot.at[x, zh, cot_half], dev(x=(x + d) % 4))
        for d in range(1, 4)
    ]
    arrive(cot_z)
    cot_far_x = [
        send(cot.at[x, oz, cot_8th], cot.at[x, oz, cot_8th], dev(x=(x + d) % 4))
        for d in range(1, 4)
    ]
    lax.fori_loop(4, 8, emb_part, 0)
    emb[...] = acc[...].astype(BF16).reshape(2, 256, 1024)
    emb_cs = [send(emb.at[oc], emb_c, dev(c=oc))]
    arrive(hid_y)
    hid_c = [send(hid.at[:, :, hid_half, :], hid.at[:, :, hid_half, :], dev(c=oc))]
    arrive(st_x)
    st_c = [send(st.at[:, :, :, st_rows_c, :], st.at[:, :, :, st_rows_c, :], dev(c=oc))]
    arrive(emb_cs)
    emb_1 = (emb[c].astype(F32) + emb_c[...].astype(F32)).astype(BF16)
    emb[c] = emb_1
    emb_ys = [
        send(
            emb.at[c, pl.ds(pl.multiple_of(((y + d) % 4) * 64, 64), 64)],
            emb_y.at[d - 1], dev(y=(y + d) % 4),
        )
        for d in range(1, 4)
    ]
    arrive(cot_far_x)
    cot_y = [
        send(cot.at[:, oz, cot_8th, :], cot.at[:, oz, cot_8th, :], dev(y=(y + d) % 4))
        for d in range(1, 4)
    ]

    arrive(hid_c)
    own_rows = tab.at[r]

    def student(p, carry):
        slog[p] = dot_nt(own_rows[...], hid[p].reshape(256, 1024))
        return carry

    lax.fori_loop(0, 4, student, 0)
    for p in range(4):
        values = slog[p]
        top = jnp.max(values, axis=0, keepdims=True)
        sstat[0, p : p + 1, :] = top
        sstat[0, 4 + p : 5 + p, :] = jnp.sum(jnp.exp(values - top), axis=0, keepdims=True)
    sst_cs = [send(sstat.at[0], sst_c, dev(c=oc))]

    arrive(emb_ys)
    mine = emb[c, pl.ds(pl.multiple_of(y * 64, 64), 64)].astype(F32)
    for d in range(3):
        mine = mine + emb_y[d].astype(F32)
    emb_2[...] = mine.astype(BF16)
    emb_zs = [
        send(
            emb_2.at[pl.ds(pl.multiple_of(((zl + d) % 4) * 16, 16), 16)],
            emb_z.at[d - 1], dev(zl=(zl + d) % 4),
        )
        for d in range(1, 4)
    ]

    arrive(sst_cs)
    sstat[1] = merge(sstat[0], [sst_c[...]])
    sst_xs = [send(sstat.at[1], sst_x.at[d - 1], dev(x=(x + d) % 4)) for d in range(1, 4)]

    arrive(st_c)
    arrive(meta_r)
    slot = lax.broadcasted_iota(jnp.int32, (512, 128), 0)
    lane_128 = lax.broadcasted_iota(jnp.int32, (512, 128), 1)

    def place(i, carry):
        px, pz = i // 2, i % 2
        rows = meta[px, pz]
        parts = [
            ((rows[4 + k : 5 + k, :] == slot % 128) & (lane_128 % 4 == slot // 128)).astype(BF16)
            for k in range(4)
        ]
        move = jnp.concatenate(parts, axis=1)
        for half in range(2):
            placed = dot_nn(move, st[half, px, pz]).astype(BF16)
            for j in range(4):
                order_st[half * 4 + j, px, pz] = placed[j * 128 : (j + 1) * 128]
        return carry

    lax.fori_loop(0, 8, place, 0)

    arrive(sst_xs)
    sstat[2] = merge(sstat[1], [sst_x[d] for d in range(3)])
    sst_ys = [send(sstat.at[2], sst_y.at[d - 1], dev(y=(y + d) % 4)) for d in range(1, 4)]

    def teacher(chunk, first):
        def one(p, carry):
            part = dot_nt(headbuf[chunk], order_st[chunk, p].reshape(256, 256))
            if first:
                tlog[p] = part
            else:
                tlog[p] += part
            return carry

        lax.fori_loop(0, 4, one, 0)

    own_head.wait()
    teacher(r, True)
    arrive(sst_ys)
    sstat[3] = merge(sstat[2], [sst_y[d] for d in range(3)])
    sst_zs = [send(sstat.at[3], sst_z.at[d - 1], zdev(d)) for d in range(1, 8)]
    for k, d in enumerate(range(1, 4)):
        head_x[k].wait_recv()
        teacher(((x + 4 - d) % 4) * 2 + zh, False)

    arrive(cot_own_x)
    arrive(cot_y)
    cot_c = [send(cot.at[:, :, cot_half, :], cot.at[:, :, cot_half, :], dev(c=oc))]

    arrive(emb_zs)
    mine = emb_2[pl.ds(pl.multiple_of(zl * 16, 16), 16)].astype(F32)
    for d in range(3):
        mine = mine + emb_z[d].astype(F32)
    emb_out[...] = (mine * 32.0).astype(BF16)

    for k, d in enumerate(range(0, 4)):
        head_z[k].wait_recv()
        teacher(((x + 4 - d) % 4) * 2 + oz, False)

    for p in range(4):
        values = tlog[p]
        top = jnp.max(values, axis=0, keepdims=True)
        weights = jnp.exp(values - top)
        tstat[0, p : p + 1, :] = top
        tstat[0, 4 + p : 5 + p, :] = jnp.sum(weights, axis=0, keepdims=True)
        tstat[0, 8 + p : 9 + p, :] = jnp.sum(weights * (values - slog[p]), axis=0, keepdims=True)
        tstat[0, 12 + p : 13 + p, :] = jnp.zeros((1, 256), F32)
    tst_cs = [send(tstat.at[0], tst_c, dev(c=oc))]
    arrive(sst_zs)
    student_total = merge(sstat[3], [sst_z[d] for d in range(7)])
    student_lse = student_total[0:4] + jnp.log(student_total[4:8])
    mask = jnp.concatenate(
        [
            jnp.concatenate([meta[p, 0, 3:4, :], meta[p, 1, 3:4, :]], axis=1).astype(F32)
            for p in range(4)
        ],
        axis=0,
    )
    mask_total = jnp.sum(mask, axis=(0, 1), keepdims=True)
    token_weight = mask * (8 * 128) / mask_total
    arrive(tst_cs)
    tstat[1] = merge(tstat[0], [tst_c[...]])
    tst_xs = [send(tstat.at[1], tst_x.at[d - 1], dev(x=(x + d) % 4)) for d in range(1, 4)]
    arrive(tst_xs)
    tstat[2] = merge(tstat[1], [tst_x[d] for d in range(3)])
    tst_ys = [send(tstat.at[2], tst_y.at[d - 1], dev(y=(y + d) % 4)) for d in range(1, 4)]
    arrive(tst_ys)
    tstat[3] = merge(tstat[2], [tst_y[d] for d in range(3)])
    tst_zs = [send(tstat.at[3], tst_z.at[d - 1], zdev(d)) for d in range(1, 8)]
    arrive(tst_zs)
    total = merge(tstat[3], [tst_z[d] for d in range(7)])
    teacher_sum = total[4:8]
    teacher_lse = total[0:4] + jnp.log(teacher_sum)

    sstat[4, 0:4, :] = student_lse
    sstat[4, 4:8, :] = token_weight
    tstat[4, 0:4, :] = teacher_lse

    def gradient(p):
        row = pl.ds(p, 1)
        student_prob = jnp.exp(slog[p] - sstat[4, row, :])
        teacher_prob = jnp.exp(tlog[p] - tstat[4, row, :])
        return (sstat[4, pl.ds(4 + p, 1), :] * (student_prob - teacher_prob)).astype(BF16)

    g_x = []
    for d in range(1, 4):
        p = (x + d) % 4
        gbuf[p] = gradient(p)
        g_x.append(send(gbuf.at[p], gx.at[x], dev(x=p)))
    own_grad = gradient(x)
    gbuf[x] = own_grad
    gx[x] = own_grad

    token_kl = total[8:12] / teacher_sum - teacher_lse + student_lse
    kl = jnp.sum(mask * token_kl, axis=(0, 1), keepdims=True) / mask_total
    kl_out[...] = jnp.broadcast_to(kl, (8, 128))

    def hidden_part(k, first):
        part = dot_tn(gx[k], tab[k * 2 + zh]).reshape(2, 2, 64, 1024)
        if first:
            hp[...] = part
        else:
            hp[...] += part

    hidden_part(x, True)
    for d in range(1, 4):
        g_x[d - 1].wait_recv()
        hidden_part((x + 4 - d) % 4, False)
    hp_cs = [send(hp.at[:, oc], hp_c, dev(c=oc))]

    def table_part(p, carry):
        part = dot_nn(gbuf[p], hid[p].reshape(256, 1024))

        @pl.when(p == 0)
        def _():
            acc[...] = part

        @pl.when(p != 0)
        def _():
            acc[...] += part

        return carry

    lax.fori_loop(0, 4, table_part, 0)
    arrive(hp_cs)
    h1[...] = (hp[:, c] + hp_c[...]).reshape(2, 4, 16, 1024)
    h1_ys = [
        send(h1.at[:, (y + d) % 4], h1_y.at[d - 1], dev(y=(y + d) % 4)) for d in range(1, 4)
    ]

    arrive(cot_c)
    base = v * 4096 + r * 512

    def lookup(i, carry):
        px, pz = i // 2, i % 2
        rows = meta[px, pz]
        onehot = jnp.concatenate(
            [(rows[k : k + 1, :] - base == slot).astype(BF16) for k in range(3)], axis=1
        )
        acc[...] += dot_nn(onehot, cot[px, pz]) * 32.0
        return carry

    lax.fori_loop(0, 4, lookup, 0)
    arrive(h1_ys)
    mine = h1[:, y]
    for d in range(3):
        mine = mine + h1_y[d]
    for i in range(4):
        h2[:, i] = mine[:, 4 * i : 4 * i + 4]
    h2_zs = []
    for d in range(1, 8):
        to = (z + d) % 8
        h2_zs.append(send(h2.at[to // 4, to % 4], h2_z.at[d - 1], zdev(d)))
    lax.fori_loop(4, 8, lookup, 0)
    tg_out[...] = acc[...].astype(BF16)
    arrive(h2_zs)
    result = h2[zh, zl]
    for d in range(7):
        result = result + h2_z[d]
    hg_out[...] = result
    for copy in pending:
        copy.wait_send()


def on_device(
    src_ids, tgt_ids, tgt_mask, tgt_order, table, student_hidden, teacher_hidden, teacher_head,
    src_embed_grad, tgt_embed_grad,
):
    first_row = lax.axis_index("vocab") * table.shape[0]

    def slots(values, n):
        return values.reshape((4, 4, 2, n) + values.shape[1:]).swapaxes(1, 2).swapaxes(0, 1)

    hidden = slots(student_hidden[0], 4).reshape(128, 1024)
    mask = slots(tgt_mask[0], 4).reshape(1, 128)
    order = slots(tgt_order[0], 4).reshape(128)
    order = (order // 4) % 2 * 64 + order // 32 * 16 + (order // 8) % 4 * 4 + order % 4
    order = jnp.repeat(order, 4).reshape(4, 128)
    meta = jnp.concatenate([src_ids[0].reshape(2, 128), tgt_ids, mask, order], axis=0)
    ids_col = jnp.concatenate(
        [
            slots(src_ids[0], 8) - first_row,
            slots(tgt_ids[0], 4) - first_row,
            jnp.full((2, 4, 4, 4), -1, jnp.int32),
        ],
        axis=3,
    ).reshape(512, 1)
    states = teacher_hidden[0].reshape(4, 2, 4, 256).swapaxes(0, 1).reshape(2, 16, 256)

    vmem = pl.BlockSpec(memory_space=pltpu.VMEM)
    hbm = pl.BlockSpec(memory_space=pl.ANY)

    def scratch(shape, dtype=BF16):
        return pltpu.VMEM(shape, dtype)

    emb, kl, hg, tg = pl.pallas_call(
        kernel,
        name="distill",
        out_shape=(
            jax.ShapeDtypeStruct((16, 1024), BF16),
            jax.ShapeDtypeStruct((8, 128), F32),
            jax.ShapeDtypeStruct((4, 1024), F32),
            jax.ShapeDtypeStruct((512, 1024), BF16),
        ),
        in_specs=[hbm, hbm, hbm, hbm, hbm, hbm, hbm, vmem],
        out_specs=(vmem, vmem, vmem, vmem),
        scratch_shapes=[
            scratch((8, 512, 1024)),
            scratch((8, 512, 256)),
            scratch((4, 2, 128, 1024)),
            scratch((4, 2, 384, 1024)),
            scratch((2, 4, 2, 512, 256)),
            scratch((4, 2, 8, 128), jnp.int32),
            scratch((8, 4, 2, 128, 256)),
            scratch((4, 512, 256), F32),
            scratch((4, 512, 256), F32),
            scratch((512, 1024), F32),
            scratch((4, 512, 256)),
            scratch((4, 512, 256)),
            scratch((2, 256, 1024)),
            scratch((64, 1024)),
            scratch((256, 1024)),
            scratch((3, 64, 1024)),
            scratch((3, 16, 1024)),
            scratch((5, 8, 256), F32),
            scratch((8, 256), F32),
            scratch((3, 8, 256), F32),
            scratch((3, 8, 256), F32),
            scratch((7, 8, 256), F32),
            scratch((5, 16, 256), F32),
            scratch((16, 256), F32),
            scratch((3, 16, 256), F32),
            scratch((3, 16, 256), F32),
            scratch((7, 16, 256), F32),
            scratch((2, 2, 64, 1024), F32),
            scratch((2, 64, 1024), F32),
            scratch((2, 4, 16, 1024), F32),
            scratch((3, 2, 16, 1024), F32),
            scratch((2, 4, 4, 1024), F32),
            scratch((7, 4, 1024), F32),
            pltpu.SemaphoreType.DMA((16,)),
            pltpu.SemaphoreType.DMA((112,)),
            pltpu.SemaphoreType.DMA((112,)),
        ],
        compiler_params=pltpu.CompilerParams(
            collective_id=0, has_side_effects=True, vmem_limit_bytes=60 * 2**20
        ),
        cost_estimate=pl.CostEstimate(
            flops=12 * 10**9, bytes_accessed=16 * 2**20, transcendentals=2 * 10**6
        ),
    )(
        teacher_head, table, hidden, src_embed_grad[0], tgt_embed_grad[0], states, meta, ids_col,
    )
    return (emb[None, 0:8], emb[None, 8:12], kl[0, 0], hg[None], tg)


def solution(mesh):
    return jax.shard_map(
        on_device,
        mesh=mesh,
        in_specs=(
            P("rep", None),
            P("rep", None),
            P("rep", None),
            P("rep", None),
            P("vocab", None),
            P("rep", None, None),
            P("rep", "vocab", None),
            P("vocab", "rep"),
            P("rep", None, None),
            P("rep", None, None),
        ),
        out_specs=(
            P("rep", "vocab", None),
            P("rep", "vocab", None),
            P(),
            P("rep", "vocab", None),
            P(("vocab", "rep"), None),
        ),
        check_vma=False,
    )
```

```python
import functools

import jax
import jax.numpy as jnp
from jax import lax
from jax.experimental import pallas as pl
from jax.experimental.pallas import tpu as pltpu
from jax.sharding import PartitionSpec as P

MESH = pl.DeviceIdType.MESH
PACK = 16
NX, NY, NZL, NZH, NC = 4, 4, 4, 2, 2
NZ = NZL * NZH
F32, BF16 = jnp.float32, jnp.bfloat16


def dot_nt(a, b):
    return lax.dot_general(a, b, (((1,), (1,)), ((), ())), preferred_element_type=F32)


def dot_nn(a, b):
    return lax.dot_general(a, b, (((1,), (0,)), ((), ())), preferred_element_type=F32)


def dot_tn(a, b):
    return lax.dot_general(a, b, (((0,), (0,)), ((), ())), preferred_element_type=F32)


def merge(own, others):
    groups = own.shape[0] // 4
    tops = [piece[0:4] for piece in [own] + others]
    top = functools.reduce(jnp.maximum, tops)
    total = [0.0] * (groups - 1)
    for piece, piece_top in zip([own] + others, tops):
        factor = jnp.exp(piece_top - top)
        for g in range(1, groups):
            total[g - 1] = total[g - 1] + piece[4 * g : 4 * g + 4] * factor
    return jnp.concatenate([top] + total, axis=0)


def kernel(
    head, table, hidden_in, src_cot, tgt_cot, states_in, src_ids, tgt_ids, tgt_mask, tgt_order,
    src_out, tgt_out, kl_out, hg_out, full_out, base, packs, meta,
    tab, headbuf, hid_raw, hid, cot, pack, st, st_f32, expand, slot_ids, order_st, slog, tlog,
    acc, gbuf, gx, emb, emb_2, emb_c, emb_y, emb_z,
    sstat, sst_1, sst_2, sst_3, tstat, tst_1, tst_2, tst_3, cstat, cst_1, cst_2, cst_3,
    hp, hp_c, h1, h1_y, h2, h2_z,
    lsem, ssem, rsem,
):
    v, r = lax.axis_index("vocab"), lax.axis_index("rep")
    y, zl, c = v // 8, (v // 2) % 4, v % 2
    x, zh = r // 2, r % 2
    z = zh * 4 + zl
    oc = 1 - c
    oz = 1 - zh

    def dev(y=y, zl=zl, c=c, x=x, zh=zh):
        return ((y * 4 + zl) * 2 + c, x * 2 + zh)

    def zdev(d):
        to = (z + d) % 8
        return dev(zl=to % 4, zh=to // 4)

    def xdev(d):
        return dev(x=(x + d) % 4)

    def ydev(d):
        return dev(y=(y + d) % 4)

    def xcdev(dx, dc):
        return dev(x=(x + dx) % 4, c=(c + dc) % 2)

    used = {"l": 0, "r": 0}
    pending = []

    def local(src, dst):
        i = used["l"]
        used["l"] += 1
        copy = pltpu.make_async_copy(src, dst, lsem.at[i])
        copy.start()
        return copy

    def send(src, dst, to):
        i = used["r"]
        used["r"] += 1
        copy = pltpu.make_async_remote_copy(
            src_ref=src, dst_ref=dst, send_sem=ssem.at[i], recv_sem=rsem.at[i],
            device_id=to, device_id_type=MESH,
        )
        copy.start()
        pending.append(copy)
        return copy

    def same(ref, to):
        return send(ref, ref, to)

    def arrive(copies):
        for copy in copies:
            copy.wait_recv()

    barrier = pltpu.get_barrier_semaphore()
    rep_offsets = [(dx, dz) for dz in (1, 0) for dx in range(4) if (dx, dz) != (0, 0)]
    xc_offsets = [(dx, dc) for dc in (0, 1) for dx in range(4) if (dx, dc) != (0, 0)]
    peers = [dev(x=(x + dx) % 4, zh=(zh + dz) % 2) for dx, dz in rep_offsets]
    peers += [zdev(d) for d in range(1, 8) if d != 4]
    peers += [ydev(d) for d in range(1, 4)]
    peers += [xcdev(dx, 1) for dx in range(4)]
    for peer in peers:
        pl.semaphore_signal(barrier, inc=1, device_id=peer, device_id_type=MESH)

    def rows(start, step, count):
        return pl.ds(pl.multiple_of(start, step), count)

    own_raw = local(hidden_in.at[0], hid_raw)
    own_head = local(head.at[rows(r * 512, 512, 512)], headbuf.at[r])
    own_cot = [
        local(src_cot.at[0], cot.at[pl.ds(0, 256)]),
        local(tgt_cot.at[0], cot.at[pl.ds(256, 128)]),
    ]
    tab_copies = [local(table.at[pl.ds(b * 512, 512)], tab.at[b]) for b in range(8)]

    st_8th = rows(c * 256 + y * 64 + zl * 16, 16, 16)
    st_y = rows(c * 256 + y * 64, 64, 64)
    st_c = rows(c * 256, 256, 256)
    for k in range(8):
        st_f32[k // 4, (k % 4) * 4 : (k % 4) * 4 + 4, :] = states_in[
            0, :, k * 256 : (k + 1) * 256
        ].astype(F32)
    for half in range(2):
        st[half, x, zh, st_8th, :] = st_f32[half].astype(BF16)
    own_slot = c * 64 + y * 16 + lax.broadcasted_iota(jnp.int32, (16, 128), 0)

    def position(s):
        return (s // 16) % 4 * 32 + (s // 4) % 4 * 8 + s // 64 * 4 + s % 4

    pick = (position(own_slot) == lax.broadcasted_iota(jnp.int32, (16, 128), 1)).astype(BF16)
    hid_8th = rows(c * 64 + y * 16, 16, 16)
    hid_half = rows(c * 64, 64, 64)
    own_raw.wait()
    hid[x, zh, hid_8th, :] = dot_nn(pick, hid_raw[...]).astype(BF16)

    pl.semaphore_wait(barrier, len(peers))

    st_zs = [same(st.at[:, x, zh, st_8th, :], zdev(d)) for d in range(1, 8)]
    hid_z = [same(hid.at[x, zh, hid_8th], dev(zh=oz))]

    def send_head(offsets):
        copies = []
        for dx, dz in offsets:
            to_x, to_zh = (x + dx) % 4, (zh + dz) % 2
            block = head.at[rows((to_x * 2 + to_zh) * 512, 512, 512)]
            copies.append(send(block, headbuf.at[r], dev(x=to_x, zh=to_zh)))
        return copies

    head_x = send_head(rep_offsets[4:])

    ids = jnp.concatenate([src_ids[...], tgt_ids[...]], axis=1)
    pieces = jnp.concatenate(
        [ids & 255, (ids >> 8) & 255, ids >> 16, jnp.zeros((13, 384), jnp.int32)], axis=0
    ).astype(F32).astype(BF16)
    s = lax.broadcasted_iota(jnp.int32, (384, 512), 1)
    source = lax.broadcasted_iota(jnp.int32, (384, 512), 0)
    e = s % 16
    chip = (s // 64) % 4 * 8 + (s // 16) % 4 * 2 + s // 256
    wanted = jnp.where(e < 8, chip * 8 + e, 256 + chip * 4 + e - 8)
    moved = dot_nn(pieces, ((wanted == source) & (e < 12)).astype(BF16))
    slot_id = (moved[0:1] + moved[1:2] * 256.0 + moved[2:3] * 65536.0).astype(jnp.int32)
    empty = lax.broadcasted_iota(jnp.int32, (1, 512), 1) % 16 >= 12
    slot_ids[...] = jnp.broadcast_to(jnp.where(empty, -1, slot_id - v * 4096), (8, 512))

    power = lax.broadcasted_iota(jnp.int32, (16, 128), 0)
    power = jnp.where(power == 0, 1, jnp.where(power == 1, 256, jnp.where(power == 2, 65536, 0)))
    id_col = dot_tn(pieces, power.astype(F32).astype(BF16)).astype(jnp.int32)[:, 0:1]
    later = lax.broadcasted_iota(jnp.int32, (384, 384), 0) < lax.broadcasted_iota(
        jnp.int32, (384, 384), 1
    )
    repeat = jnp.max(
        jnp.where((id_col == ids) & later, 1, 0), axis=0, keepdims=True
    )
    ahead = ((id_col >> 9) == (ids >> 9)) & (ids < id_col) & (repeat == 0)
    place_col = jnp.sum(jnp.where(ahead, 1, 0), axis=1, keepdims=True)
    target = lax.broadcasted_iota(jnp.int32, (384, 128), 1)
    chosen = ((id_col >> 9) == v * 8 + target // PACK) & (place_col == target % PACK)
    row_lane = jnp.max(jnp.where(chosen, id_col & 511, -1), axis=0, keepdims=True)
    for copy in own_cot:
        copy.wait()
    pack[...] = dot_tn(chosen.astype(F32).astype(BF16), cot[...]).reshape(8, PACK, 1024)
    packs[r] = pack[r]
    fullest = jnp.max(place_col, axis=(0, 1), keepdims=True)
    meta[x, zh] = jnp.concatenate(
        [
            src_ids[:, 0:128], src_ids[:, 128:256], tgt_ids[...], tgt_mask[...], tgt_order[...],
            row_lane, jnp.broadcast_to(fullest, (1, 128)), jnp.zeros((1, 128), jnp.int32),
        ],
        axis=0,
    )
    meta_r = [
        same(meta.at[x, zh], dev(x=(x + dx) % 4, zh=(zh + dz) % 2)) for dx, dz in rep_offsets
    ]

    def send_pack(offsets):
        copies = []
        for dx, dz in offsets:
            to_x, to_zh = (x + dx) % 4, (zh + dz) % 2
            copies.append(send(pack.at[to_x * 2 + to_zh], packs.at[r], dev(x=to_x, zh=to_zh)))
        return copies

    packs_x = send_pack(rep_offsets[4:])

    row_512 = lax.broadcasted_iota(jnp.int32, (512, 512), 0)

    def emb_part(b, carry):
        onehot = (slot_ids[0:1, :] == row_512 + b * 512).astype(BF16)
        part = dot_tn(onehot, tab[b])

        @pl.when(b == 0)
        def _():
            acc[...] = part

        @pl.when(b != 0)
        def _():
            acc[...] += part

        return carry

    for copy in tab_copies:
        copy.wait()

    def st_y_of(d):
        return rows(c * 256 + (y + 4 - d) % 4 * 64, 64, 64)

    def hid_8th_of(d):
        return rows(c * 64 + (y + 4 - d) % 4 * 16, 16, 16)

    arrive(st_zs)
    st_ya = [same(st.at[0, x, :, st_y, :], ydev(d)) for d in range(1, 4)]
    st_xb = [same(st.at[1, x, :, st_y, :], xdev(d)) for d in range(1, 4)]
    head_z = send_head(rep_offsets[:4])
    arrive(hid_z)
    hid_x = [same(hid.at[x, :, hid_8th, :], xdev(d)) for d in range(1, 4)]
    arrive(st_ya)
    st_xa = [same(st.at[0, x, :, st_c, :], xdev(d)) for d in range(1, 4)]
    arrive(st_xb)
    st_yb = [same(st.at[1, :, :, st_y, :], ydev(d)) for d in range(1, 4)]
    to_core = [
        same(st.at[0, x, :, st_c, :], dev(c=oc)),
        same(st.at[1, :, :, st_y, :], dev(c=oc)),
    ]
    lax.fori_loop(0, 2, emb_part, 0)
    arrive(hid_x)
    hid_y = [same(hid.at[:, :, hid_8th, :], ydev(d)) for d in range(1, 4)]
    hid_c = [same(hid.at[:, :, hid_8th, :], dev(c=oc))]
    lax.fori_loop(2, 5, emb_part, 0)
    for k, d in enumerate((1, 3, 2)):
        arrive([st_xa[d - 1]])
        to_core.append(same(st.at[0, (x + 4 - d) % 4, :, st_c, :], dev(c=oc)))
        arrive([st_yb[d - 1]])
        to_core.append(same(st.at[1, :, :, st_y_of(d), :], dev(c=oc)))
    for d in (1, 3, 2):
        arrive([hid_y[d - 1]])
        hid_c.append(same(hid.at[:, :, hid_8th_of(d), :], dev(c=oc)))
    lax.fori_loop(5, 8, emb_part, 0)
    emb[...] = acc[...].astype(BF16).reshape(2, 256, 1024)
    emb_cs = [send(emb.at[oc], emb_c, dev(c=oc))]

    k_lane = lax.broadcasted_iota(jnp.int32, (128, 512), 1)
    arrival = (k_lane // 64) % 4 * 32 + (k_lane // 16) % 4 * 8 + k_lane // 256 * 4 + k_lane % 4
    expand[...] = (lax.broadcasted_iota(jnp.int32, (128, 512), 0) == arrival).astype(BF16)
    slot = lax.broadcasted_iota(jnp.int32, (512, 512), 0)
    column = lax.broadcasted_iota(jnp.int32, (512, 512), 1)
    arrive(meta_r)
    arrive(to_core)

    def place(i, carry):
        px, pz = i // 2, i % 2
        order = meta[px, pz]
        order = (order // 4) % 2 * 64 + (order // 32) * 16 + (order // 8) % 4 * 4 + order % 4
        order = dot_nn(order.astype(F32).astype(BF16), expand[...])[4:5].astype(jnp.int32)
        move = ((order == slot % 128) & (column // 4 % 4 == slot // 128)).astype(BF16)
        for half in range(2):
            placed = dot_nn(move, st[half, px, pz]).astype(BF16)
            for j in range(4):
                order_st[half * 4 + j, px, pz] = placed[j * 128 : (j + 1) * 128]
        return carry

    lax.fori_loop(0, 8, place, 0)

    arrive(hid_c)
    own_rows = tab.at[r]

    def student(p, carry):
        slog[p] = dot_nt(own_rows[...], hid[p].reshape(256, 1024))
        return carry

    lax.fori_loop(0, 4, student, 0)
    for p in range(4):
        values = slog[p]
        top = jnp.max(values, axis=0, keepdims=True)
        sstat[0, p : p + 1, :] = top
        sstat[0, 4 + p : 5 + p, :] = jnp.sum(jnp.exp(values - top), axis=0, keepdims=True)

    def share_xc(stat, into):
        return [
            send(stat.at[0], into.at[k], xcdev(dx, dc)) for k, (dx, dc) in enumerate(xc_offsets)
        ]

    def share_y(stat, into):
        return [send(stat.at[1], into.at[d - 1], ydev(d)) for d in range(1, 4)]

    def share_z(stat, into):
        return [send(stat.at[2], into.at[d - 1], zdev(d)) for d in range(1, 8)]

    def merged(copies, stat, level, into):
        arrive(copies)
        return merge(stat[level], [into[k] for k in range(len(copies))])

    sst_1s = share_xc(sstat, sst_1)
    arrive(emb_cs)
    emb[c] = (emb[c].astype(F32) + emb_c[...].astype(F32)).astype(BF16)
    emb_ys = [
        send(emb.at[c, rows(((y + d) % 4) * 64, 64, 64)], emb_y.at[d - 1], ydev(d))
        for d in range(1, 4)
    ]

    def teacher(chunk, first):
        def one(p, carry):
            part = dot_nt(headbuf[chunk], order_st[chunk, p].reshape(256, 256))
            if first:
                tlog[p] = part
            else:
                tlog[p] += part
            return carry

        lax.fori_loop(0, 4, one, 0)

    own_head.wait()
    teacher(r, True)
    sstat[1] = merged(sst_1s, sstat, 0, sst_1)
    sst_2s = share_y(sstat, sst_2)
    for k, d in enumerate(range(1, 4)):
        arrive([head_x[k]])
        teacher(((x + 4 - d) % 4) * 2 + zh, False)
    sstat[2] = merged(sst_2s, sstat, 1, sst_2)
    sst_3s = share_z(sstat, sst_3)
    arrive(emb_ys)
    mine = emb[c, rows(y * 64, 64, 64)].astype(F32)
    for d in range(3):
        mine = mine + emb_y[d].astype(F32)
    emb_2[...] = mine.astype(BF16)
    emb_zs = [
        send(emb_2.at[rows(((zl + d) % 4) * 16, 16, 16)], emb_z.at[d - 1], dev(zl=(zl + d) % 4))
        for d in range(1, 4)
    ]

    student_total = merged(sst_3s, sstat, 2, sst_3)
    student_lse = student_total[0:4] + jnp.log(student_total[4:8])
    mask = jnp.concatenate([meta[i // 2, i % 2, 3:4, :] for i in range(8)], axis=0)
    to_slot = position(lax.broadcasted_iota(jnp.int32, (128, 128), 1)) == lax.broadcasted_iota(
        jnp.int32, (128, 128), 0
    )
    mask = dot_nn(mask.astype(F32).astype(BF16), to_slot.astype(BF16))
    mask = jnp.concatenate(
        [jnp.concatenate([mask[2 * p : 2 * p + 1], mask[2 * p + 1 : 2 * p + 2]], axis=1) for p in range(4)],
        axis=0,
    )
    mask_total = jnp.sum(mask, axis=(0, 1), keepdims=True)
    sstat[3, 0:4, :] = student_lse
    sstat[3, 4:8, :] = mask * (8 * 128) / mask_total

    for k, d in enumerate(range(0, 4)):
        arrive([head_z[k]])
        teacher(((x + 4 - d) % 4) * 2 + oz, False)

    for p in range(4):
        values = tlog[p]
        top = jnp.max(values, axis=0, keepdims=True)
        weights = jnp.exp(values - top)
        tstat[0, p : p + 1, :] = top
        tstat[0, 4 + p : 5 + p, :] = jnp.sum(weights, axis=0, keepdims=True)
        cstat[0, p : p + 1, :] = top
        cstat[0, 4 + p : 5 + p, :] = jnp.sum(weights * (values - slog[p]), axis=0, keepdims=True)
    tst_1s = share_xc(tstat, tst_1)
    tstat[1] = merged(tst_1s, tstat, 0, tst_1)
    tst_2s = share_y(tstat, tst_2)
    tstat[2] = merged(tst_2s, tstat, 1, tst_2)
    tst_3s = share_z(tstat, tst_3)
    total = merged(tst_3s, tstat, 2, tst_3)
    teacher_lse = total[0:4] + jnp.log(total[4:8])
    tstat[3, 0:4, :] = teacher_lse
    tstat[3, 4:8, :] = total[4:8]

    def gradient(p):
        row = pl.ds(p, 1)
        student_prob = jnp.exp(slog[p] - sstat[3, row, :])
        teacher_prob = jnp.exp(tlog[p] - tstat[3, row, :])
        return (sstat[3, pl.ds(4 + p, 1), :] * (student_prob - teacher_prob)).astype(BF16)

    packs_z = send_pack(rep_offsets[:4])
    g_x = []
    for d in range(1, 4):
        p = (x + d) % 4
        gbuf[p] = gradient(p)
        g_x.append(send(gbuf.at[p], gx.at[x], xdev(d)))
    own_grad = gradient(x)
    gbuf[x] = own_grad
    gx[x] = own_grad
    cst_1s = share_xc(cstat, cst_1)

    arrive(emb_zs)
    mine = emb_2[rows(zl * 16, 16, 16)].astype(F32)
    for d in range(3):
        mine = mine + emb_z[d].astype(F32)
    mine = (mine * 32.0).astype(BF16)
    src_out[0] = mine[0:8]
    tgt_out[0] = mine[8:12]

    def hidden_part(k, first):
        part = dot_tn(gx[k], tab[k * 2 + zh]).reshape(2, 2, 64, 1024)
        if first:
            hp[...] = part
        else:
            hp[...] += part

    hidden_part(x, True)
    for d in range(1, 4):
        arrive([g_x[d - 1]])
        hidden_part((x + 4 - d) % 4, False)
    hp_cs = [send(hp.at[:, oc], hp_c, dev(c=oc))]
    cstat[1] = merged(cst_1s, cstat, 0, cst_1)
    cst_2s = share_y(cstat, cst_2)

    def table_part(p, carry):
        part = dot_nn(gbuf[p], hid[p].reshape(256, 1024))

        @pl.when(p == 0)
        def _():
            base[...] = part

        @pl.when(p != 0)
        def _():
            base[...] += part

        return carry

    lax.fori_loop(0, 4, table_part, 0)
    arrive(hp_cs)
    h1[...] = (hp[:, c] + hp_c[...]).reshape(2, 4, 16, 1024)
    h1_ys = [send(h1.at[:, (y + d) % 4], h1_y.at[d - 1], ydev(d)) for d in range(1, 4)]

    cstat[2] = merged(cst_2s, cstat, 1, cst_2)
    cst_3s = share_z(cstat, cst_3)
    arrive(h1_ys)
    mine = h1[:, y]
    for d in range(3):
        mine = mine + h1_y[d]
    for i in range(4):
        h2[:, i] = mine[:, 4 * i : 4 * i + 4]
    h2_zs = []
    for d in range(1, 8):
        to = (z + d) % 8
        h2_zs.append(send(h2.at[to // 4, to % 4], h2_z.at[d - 1], zdev(d)))
    arrive(packs_x)
    arrive(packs_z)
    cross = merged(cst_3s, cstat, 2, cst_3)
    token_kl = cross[4:8] / tstat[3, 4:8, :] - tstat[3, 0:4, :] + sstat[3, 0:4, :]
    weight = sstat[3, 4:8, :]
    kl = jnp.sum(weight * token_kl, axis=(0, 1), keepdims=True) / (8 * 128)
    kl_out[...] = kl
    fullest = [meta[i // 2, i % 2, 6:7, 0:1] for i in range(8)]
    full_out[...] = functools.reduce(jnp.maximum, fullest)
    arrive(h2_zs)
    result = h2[zh, zl]
    for d in range(7):
        result = result + h2_z[d]
    hg_out[0] = result
    for copy in pending:
        copy.wait_send()


def add_packed(base, packs, meta, out):
    r = lax.axis_index("rep")
    owned = jnp.concatenate([meta[i // 2, i % 2, 5:6, :] for i in range(8)], axis=0) + 1
    sub_128 = lax.broadcasted_iota(jnp.int32, (128, 128), 0)
    lane_128 = lax.broadcasted_iota(jnp.int32, (128, 128), 1)
    own_slots = (sub_128 == r * PACK + lane_128 % PACK).astype(F32).astype(BF16)
    owned = dot_nn((owned & 255).astype(F32).astype(BF16), own_slots) + 256.0 * dot_nn(
        (owned >> 8).astype(F32).astype(BF16), own_slots
    )
    owned = jnp.where(sub_128[0:8] == lane_128[0:8] // PACK, owned, 0.0)
    owned = jnp.sum(owned, axis=0, keepdims=True).astype(jnp.int32) - 1
    spread = (owned == lax.broadcasted_iota(jnp.int32, (512, 128), 0)).astype(BF16)
    terms = packs[...].reshape(128, 1024)
    coarse = terms.astype(BF16)
    fine = (terms - coarse.astype(F32)).astype(BF16)
    lookup = dot_nn(spread, coarse) + dot_nn(spread, fine)
    out[...] = (base[...] + lookup * 32.0).astype(BF16)


def add_dense(base, src_cot, tgt_cot, meta, out, cots, total, lsem, ssem, rsem):
    v, r = lax.axis_index("vocab"), lax.axis_index("rep")
    copies = [
        pltpu.make_async_copy(src_cot.at[0], cots.at[r, pl.ds(0, 256)], lsem.at[0]),
        pltpu.make_async_copy(tgt_cot.at[0], cots.at[r, pl.ds(256, 128)], lsem.at[1]),
    ]
    for copy in copies:
        copy.start()
    barrier = pltpu.get_barrier_semaphore()
    peers = [(v, (r + d) % 8) for d in range(1, 8)]
    for peer in peers:
        pl.semaphore_signal(barrier, inc=1, device_id=peer, device_id_type=MESH)
    pl.semaphore_wait(barrier, 7)
    for copy in copies:
        copy.wait()
    sends = []
    for k, peer in enumerate(peers):
        sends.append(
            pltpu.make_async_remote_copy(
                src_ref=cots.at[r], dst_ref=cots.at[r], send_sem=ssem.at[k], recv_sem=rsem.at[k],
                device_id=peer, device_id_type=MESH,
            )
        )
        sends[-1].start()
    for copy in sends:
        copy.wait()
    total[...] = base[...]
    row = lax.broadcasted_iota(jnp.int32, (512, 128), 0) + (v * 4096 + r * 512)

    def one(i, carry):
        ids = meta[i // 2, i % 2]
        onehot = jnp.concatenate(
            [(ids[k : k + 1, :] == row).astype(BF16) for k in range(3)], axis=1
        )
        total[...] += dot_nn(onehot, cots[i]) * 32.0
        return carry

    lax.fori_loop(0, 8, one, 0)
    out[...] = total[...].astype(BF16)


def hand_over(*refs):
    half = len(refs) // 2
    for src, dst in zip(refs[:half], refs[half:]):
        dst[...] = src[...]


def on_device(
    src_ids, tgt_ids, tgt_mask, tgt_order, table, student_hidden, teacher_hidden, teacher_head,
    src_embed_grad, tgt_embed_grad,
):
    vmem = pl.BlockSpec(memory_space=pltpu.VMEM)
    hbm = pl.BlockSpec(memory_space=pl.ANY)

    def scratch(shape, dtype=BF16):
        return pltpu.VMEM(shape, dtype)

    def stats():
        return [
            scratch((4, 8, 256), F32), scratch((7, 8, 256), F32), scratch((3, 8, 256), F32),
            scratch((7, 8, 256), F32),
        ]

    outs = (
        jax.ShapeDtypeStruct((1, 8, 1024), BF16),
        jax.ShapeDtypeStruct((1, 4, 1024), BF16),
        jax.ShapeDtypeStruct((1, 1), F32),
        jax.ShapeDtypeStruct((1, 4, 1024), F32),
    )
    table_out = jax.ShapeDtypeStruct((512, 1024), BF16)
    results = pl.pallas_call(
        kernel,
        name="distill",
        out_shape=outs
        + (
            jax.ShapeDtypeStruct((1, 1), jnp.int32),
            jax.ShapeDtypeStruct((512, 1024), F32),
            jax.ShapeDtypeStruct((8, PACK, 1024), F32),
            jax.ShapeDtypeStruct((4, 2, 8, 128), jnp.int32),
        ),
        in_specs=[hbm, hbm, hbm, hbm, hbm, vmem, vmem, vmem, vmem, vmem],
        out_specs=(vmem,) * 8,
        scratch_shapes=[
            scratch((8, 512, 1024)),
            scratch((8, 512, 256)),
            scratch((128, 1024)),
            scratch((4, 2, 128, 1024)),
            scratch((384, 1024)),
            scratch((8, PACK, 1024), F32),
            scratch((2, 4, 2, 512, 256)),
            scratch((2, 16, 256), F32),
            scratch((128, 512)),
            scratch((8, 512), jnp.int32),
            scratch((8, 4, 2, 128, 256)),
            scratch((4, 512, 256), F32),
            scratch((4, 512, 256), F32),
            scratch((512, 1024), F32),
            scratch((4, 512, 256)),
            scratch((4, 512, 256)),
            scratch((2, 256, 1024)),
            scratch((64, 1024)),
            scratch((256, 1024)),
            scratch((3, 64, 1024)),
            scratch((3, 16, 1024)),
            *stats(),
            *stats(),
            *stats(),
            scratch((2, 2, 64, 1024), F32),
            scratch((2, 64, 1024), F32),
            scratch((2, 4, 16, 1024), F32),
            scratch((3, 2, 16, 1024), F32),
            scratch((2, 4, 4, 1024), F32),
            scratch((7, 4, 1024), F32),
            pltpu.SemaphoreType.DMA((16,)),
            pltpu.SemaphoreType.DMA((144,)),
            pltpu.SemaphoreType.DMA((144,)),
        ],
        compiler_params=pltpu.CompilerParams(
            collective_id=0, has_side_effects=True, vmem_limit_bytes=60 * 2**20
        ),
        cost_estimate=pl.CostEstimate(
            flops=12 * 10**9, bytes_accessed=16 * 2**20, transcendentals=2 * 10**6
        ),
    )(
        teacher_head, table, student_hidden, src_embed_grad, tgt_embed_grad, teacher_hidden,
        src_ids, tgt_ids, tgt_mask, tgt_order,
    )
    *results, fullest, base, packs, meta = results

    def packed_path(base, packs, meta):
        return pl.pallas_call(
            add_packed, name="add_packed", out_shape=table_out, in_specs=[vmem] * 3, out_specs=vmem,
        )(base, packs, meta)

    def dense_path(base, packs, meta):
        return pl.pallas_call(
            add_dense,
            name="add_dense",
            out_shape=table_out,
            in_specs=[vmem, hbm, hbm, vmem],
            out_specs=vmem,
            scratch_shapes=[
                scratch((8, 384, 1024)),
                scratch((512, 1024), F32),
                pltpu.SemaphoreType.DMA((2,)),
                pltpu.SemaphoreType.DMA((7,)),
                pltpu.SemaphoreType.DMA((7,)),
            ],
            compiler_params=pltpu.CompilerParams(
                collective_id=1, has_side_effects=True, vmem_limit_bytes=40 * 2**20
            ),
        )(base, src_embed_grad, tgt_embed_grad, meta)

    table_grad = lax.cond(fullest[0, 0] < PACK, packed_path, dense_path, base, packs, meta)
    src, tgt, kl, hidden_grad = pl.pallas_call(
        hand_over, name="hand_over", out_shape=outs, in_specs=[vmem] * 4, out_specs=(vmem,) * 4
    )(*results)
    return (src, tgt, kl[0, 0], hidden_grad, table_grad)


def solution(mesh):
    return jax.shard_map(
        on_device,
        mesh=mesh,
        in_specs=(
            P("rep", None),
            P("rep", None),
            P("rep", None),
            P("rep", None),
            P("vocab", None),
            P("rep", None, None),
            P("rep", "vocab", None),
            P("vocab", "rep"),
            P("rep", None, None),
            P("rep", None, None),
        ),
        out_specs=(
            P("rep", "vocab", None),
            P("rep", "vocab", None),
            P(),
            P("rep", "vocab", None),
            P(("vocab", "rep"), None),
        ),
        check_vma=False,
    )
```

```python
import functools

import jax
import jax.numpy as jnp
from jax import lax
from jax.experimental import pallas as pl
from jax.experimental.pallas import tpu as pltpu
from jax.sharding import PartitionSpec as P

MESH = pl.DeviceIdType.MESH
PACK = 16
NX, NY, NZL, NZH, NC = 4, 4, 4, 2, 2
NZ = NZL * NZH
F32, BF16 = jnp.float32, jnp.bfloat16


def dot_nt(a, b):
    return lax.dot_general(a, b, (((1,), (1,)), ((), ())), preferred_element_type=F32)


def dot_nn(a, b):
    return lax.dot_general(a, b, (((1,), (0,)), ((), ())), preferred_element_type=F32)


def dot_tn(a, b):
    return lax.dot_general(a, b, (((0,), (0,)), ((), ())), preferred_element_type=F32)


def merge(own, others):
    groups = own.shape[0] // 4
    tops = [piece[0:4] for piece in [own] + others]
    top = functools.reduce(jnp.maximum, tops)
    total = [0.0] * (groups - 1)
    for piece, piece_top in zip([own] + others, tops):
        factor = jnp.exp(piece_top - top)
        for g in range(1, groups):
            total[g - 1] = total[g - 1] + piece[4 * g : 4 * g + 4] * factor
    return jnp.concatenate([top] + total, axis=0)


def kernel(
    head, table, hidden_in, src_cot, tgt_cot, states_in, src_ids, tgt_ids, tgt_mask, tgt_order,
    src_out, tgt_out, kl_out, hg_out, full_out, base, packs, meta,
    tab, headbuf, hid_raw, hid, cot, pack, st, st_f32, slot_ids, orders, order_st, slog, tlog,
    acc, gbuf, gx, emb, emb_2, emb_c, emb_y, emb_z,
    sstat, sst_1, sst_2, sst_3, tstat, tst_1, tst_2, tst_3, cstat, cst_1, cst_2, cst_3,
    hp, hp_c, h1, h1_y, h2, h2_z,
    lsem, ssem, rsem,
):
    v, r = lax.axis_index("vocab"), lax.axis_index("rep")
    y, zl, c = v // 8, (v // 2) % 4, v % 2
    x, zh = r // 2, r % 2
    z = zh * 4 + zl
    oc = 1 - c
    oz = 1 - zh

    def dev(y=y, zl=zl, c=c, x=x, zh=zh):
        return ((y * 4 + zl) * 2 + c, x * 2 + zh)

    def zdev(d):
        to = (z + d) % 8
        return dev(zl=to % 4, zh=to // 4)

    def xdev(d):
        return dev(x=(x + d) % 4)

    def ydev(d):
        return dev(y=(y + d) % 4)

    def xcdev(dx, dc):
        return dev(x=(x + dx) % 4, c=(c + dc) % 2)

    used = {"l": 0, "r": 0}
    pending = []

    def local(src, dst):
        i = used["l"]
        used["l"] += 1
        copy = pltpu.make_async_copy(src, dst, lsem.at[i])
        copy.start()
        return copy

    def send(src, dst, to):
        i = used["r"]
        used["r"] += 1
        copy = pltpu.make_async_remote_copy(
            src_ref=src, dst_ref=dst, send_sem=ssem.at[i], recv_sem=rsem.at[i],
            device_id=to, device_id_type=MESH,
        )
        copy.start()
        pending.append(copy)
        return copy

    def same(ref, to):
        return send(ref, ref, to)

    def arrive(copies):
        for copy in copies:
            copy.wait_recv()

    barrier = pltpu.get_barrier_semaphore()
    rep_offsets = [(dx, dz) for dz in (1, 0) for dx in range(4) if (dx, dz) != (0, 0)]
    xc_offsets = [(dx, dc) for dc in (0, 1) for dx in range(4) if (dx, dc) != (0, 0)]
    peers = [dev(x=(x + dx) % 4, zh=(zh + dz) % 2) for dx, dz in rep_offsets]
    peers += [zdev(d) for d in range(1, 8) if d != 4]
    peers += [ydev(d) for d in range(1, 4)]
    peers += [xcdev(dx, 1) for dx in range(4)]
    for peer in peers:
        pl.semaphore_signal(barrier, inc=1, device_id=peer, device_id_type=MESH)

    def rows(start, step, count):
        return pl.ds(pl.multiple_of(start, step), count)

    x_cols = rows(x * 256, 256, 256)
    own_raw = local(hidden_in.at[0], hid_raw)
    own_head = local(head.at[rows(r * 512, 512, 512)], headbuf.at[0, :, x_cols])
    own_cot = [
        local(src_cot.at[0], cot.at[pl.ds(0, 256)]),
        local(tgt_cot.at[0], cot.at[pl.ds(256, 128)]),
    ]
    tab_copies = [local(table.at[pl.ds(b * 512, 512)], tab.at[b]) for b in range(8)]

    st_8th = rows(c * 256 + y * 64 + zl * 16, 16, 16)
    st_y = rows(c * 256 + y * 64, 64, 64)
    st_c = rows(c * 256, 256, 256)
    for k in range(8):
        st_f32[k // 4, (k % 4) * 4 : (k % 4) * 4 + 4, :] = states_in[
            0, :, k * 256 : (k + 1) * 256
        ].astype(F32)
    for half in range(2):
        st[half, x, zh, st_8th, :] = st_f32[half].astype(BF16)
    own_slot = c * 64 + y * 16 + lax.broadcasted_iota(jnp.int32, (16, 128), 0)

    def position(s):
        return (s // 16) % 4 * 32 + (s // 4) % 4 * 8 + s // 64 * 4 + s % 4

    pick = (position(own_slot) == lax.broadcasted_iota(jnp.int32, (16, 128), 1)).astype(BF16)
    hid_8th = rows(c * 64 + y * 16, 16, 16)
    hid_half = rows(c * 64, 64, 64)
    own_raw.wait()
    hid[x, zh, hid_8th, :] = dot_nn(pick, hid_raw[...]).astype(BF16)

    pl.semaphore_wait(barrier, len(peers))

    st_zs = [same(st.at[:, x, zh, st_8th, :], zdev(d)) for d in range(1, 8)]
    hid_z = [same(hid.at[x, zh, hid_8th], dev(zh=oz))]

    def send_head(offsets):
        copies = []
        for dx, dz in offsets:
            to_x, to_zh = (x + dx) % 4, (zh + dz) % 2
            block = head.at[rows((to_x * 2 + to_zh) * 512, 512, 512)]
            copies.append(send(block, headbuf.at[dz, :, x_cols], dev(x=to_x, zh=to_zh)))
        return copies


    def st_y_of(d):
        return rows(c * 256 + (y + 4 - d) % 4 * 64, 64, 64)

    def hid_8th_of(d):
        return rows(c * 64 + (y + 4 - d) % 4 * 16, 16, 16)

    arrive(st_zs)
    st_ya = [same(st.at[0, x, :, st_y, :], ydev(d)) for d in range(1, 4)]
    st_xb = [same(st.at[1, x, :, st_y, :], xdev(d)) for d in range(1, 4)]
    head_z = send_head(rep_offsets[:4])
    arrive(hid_z)
    hid_x = [same(hid.at[x, :, hid_8th, :], xdev(d)) for d in range(1, 4)]
    arrive(st_ya)
    st_xa = [same(st.at[0, x, :, st_c, :], xdev(d)) for d in range(1, 4)]
    arrive(st_xb)
    st_yb = [same(st.at[1, :, :, st_y, :], ydev(d)) for d in range(1, 4)]
    head_x = send_head(rep_offsets[4:])
    to_core = [
        same(st.at[0, x, :, st_c, :], dev(c=oc)),
        same(st.at[1, :, :, st_y, :], dev(c=oc)),
    ]
    ids = jnp.concatenate([src_ids[...], tgt_ids[...]], axis=1)
    pieces = jnp.concatenate(
        [ids & 255, (ids >> 8) & 255, ids >> 16, jnp.zeros((13, 384), jnp.int32)], axis=0
    ).astype(F32).astype(BF16)
    s = lax.broadcasted_iota(jnp.int32, (384, 512), 1)
    source = lax.broadcasted_iota(jnp.int32, (384, 512), 0)
    e = s % 16
    chip = (s // 64) % 4 * 8 + (s // 16) % 4 * 2 + s // 256
    wanted = jnp.where(e < 8, chip * 8 + e, 256 + chip * 4 + e - 8)
    moved = dot_nn(pieces, ((wanted == source) & (e < 12)).astype(BF16))
    power = lax.broadcasted_iota(jnp.int32, (16, 128), 0)
    power = jnp.where(power == 0, 1, jnp.where(power == 1, 256, jnp.where(power == 2, 65536, 0)))
    power = power.astype(F32).astype(BF16)
    slot_id = dot_tn(moved.astype(BF16), power).astype(jnp.int32) - v * 4096
    empty = lax.broadcasted_iota(jnp.int32, (512, 128), 0) % 16 >= 12
    slot_ids[...] = jnp.where(empty, -1, slot_id)

    id_col = dot_tn(pieces, power).astype(jnp.int32)[:, 0:1]
    later = lax.broadcasted_iota(jnp.int32, (384, 384), 0) < lax.broadcasted_iota(
        jnp.int32, (384, 384), 1
    )
    repeat = jnp.max(
        jnp.where((id_col == ids) & later, 1, 0), axis=0, keepdims=True
    )
    ahead = ((id_col >> 9) == (ids >> 9)) & (ids < id_col) & (repeat == 0)
    place_col = jnp.sum(jnp.where(ahead, 1, 0), axis=1, keepdims=True)
    target = lax.broadcasted_iota(jnp.int32, (384, 128), 1)
    chosen = ((id_col >> 9) == v * 8 + target // PACK) & (place_col == target % PACK)
    row_lane = jnp.max(jnp.where(chosen, id_col & 511, -1), axis=0, keepdims=True)
    for copy in own_cot:
        copy.wait()
    pack[...] = dot_tn(chosen.astype(F32).astype(BF16), cot[...]).reshape(8, PACK, 1024)
    packs[r] = pack[r]
    fullest = jnp.max(place_col, axis=(0, 1), keepdims=True)
    meta[x, zh] = jnp.concatenate(
        [
            src_ids[:, 0:128], src_ids[:, 128:256], tgt_ids[...], tgt_mask[...], tgt_order[...],
            row_lane, jnp.broadcast_to(fullest, (1, 128)), jnp.zeros((1, 128), jnp.int32),
        ],
        axis=0,
    )
    meta_r = [
        same(meta.at[x, zh], dev(x=(x + dx) % 4, zh=(zh + dz) % 2)) for dx, dz in rep_offsets
    ]

    def send_pack(offsets):
        copies = []
        for dx, dz in offsets:
            to_x, to_zh = (x + dx) % 4, (zh + dz) % 2
            copies.append(send(pack.at[to_x * 2 + to_zh], packs.at[r], dev(x=to_x, zh=to_zh)))
        return copies

    packs_x = send_pack(rep_offsets[4:])

    row_lane_512 = lax.broadcasted_iota(jnp.int32, (512, 512), 1)

    def emb_part(b, carry):
        onehot = (slot_ids[:, 0:1] - b * 512 == row_lane_512).astype(BF16)
        part = dot_nn(onehot, tab[b])

        @pl.when(b == 0)
        def _():
            acc[...] = part

        @pl.when(b != 0)
        def _():
            acc[...] += part

        return carry

    for copy in tab_copies:
        copy.wait()
    lax.fori_loop(0, 1, emb_part, 0)
    arrive(hid_x)
    hid_y = [same(hid.at[:, :, hid_8th, :], ydev(d)) for d in range(1, 4)]
    hid_c = [same(hid.at[:, :, hid_8th, :], dev(c=oc))]
    for k, d in enumerate((1, 3, 2)):
        arrive([st_xa[d - 1]])
        to_core.append(same(st.at[0, (x + 4 - d) % 4, :, st_c, :], dev(c=oc)))
        arrive([st_yb[d - 1]])
        to_core.append(same(st.at[1, :, :, st_y_of(d), :], dev(c=oc)))
    for d in (1, 3, 2):
        arrive([hid_y[d - 1]])
        hid_c.append(same(hid.at[:, :, hid_8th_of(d), :], dev(c=oc)))

    k_lane = lax.broadcasted_iota(jnp.int32, (128, 512), 1)
    arrival = (k_lane // 64) % 4 * 32 + (k_lane // 16) % 4 * 8 + k_lane // 256 * 4 + k_lane % 4
    expand = (lax.broadcasted_iota(jnp.int32, (128, 512), 0) == arrival).astype(BF16)
    arrive(meta_r)
    order = jnp.concatenate([meta[i // 2, i % 2, 4:5, :] for i in range(8)], axis=0)
    order = (order // 4) % 2 * 64 + (order // 32) * 16 + (order // 8) % 4 * 4 + order % 4
    orders[...] = dot_nn(order.astype(F32).astype(BF16), expand).astype(jnp.int32)
    slot = lax.broadcasted_iota(jnp.int32, (128, 512), 0)
    part = lax.broadcasted_iota(jnp.int32, (128, 512), 1) // 4 % 4
    arrive(to_core)

    def place(i, carry):
        px, pz = i // 2, i % 2
        order = orders[pl.ds(i, 1), :]
        hit = jnp.where(order == slot, part, -1)
        move = jnp.concatenate([(hit == j).astype(BF16) for j in range(4)], axis=0)
        for half in range(2):
            placed = dot_nn(move, st[half, px, pz]).astype(BF16)
            for j in range(4):
                block = half * 4 + j
                order_st[
                    (zh + block) % 2, px, pz, :, block // 2 * 256 : block // 2 * 256 + 256
                ] = placed[j * 128 : (j + 1) * 128]
        return carry

    lax.fori_loop(0, 8, place, 0)

    def teacher(half, p):
        return dot_nt(headbuf[half], order_st[half, p].reshape(256, 1024))

    def teacher_near(p, carry):
        tlog[p] = teacher(0, p)
        return carry

    own_head.wait()
    arrive(head_x)
    lax.fori_loop(0, 4, teacher_near, 0)

    arrive(hid_c)
    own_rows = tab.at[r]

    def student(p, carry):
        slog[p] = dot_nt(own_rows[...], hid[p].reshape(256, 1024))
        return carry

    lax.fori_loop(0, 4, student, 0)
    for p in range(4):
        values = slog[p]
        top = jnp.max(values, axis=0, keepdims=True)
        sstat[0, p : p + 1, :] = top
        sstat[0, 4 + p : 5 + p, :] = jnp.sum(jnp.exp(values - top), axis=0, keepdims=True)

    def share_xc(stat, into):
        return [
            send(stat.at[0], into.at[k], xcdev(dx, dc)) for k, (dx, dc) in enumerate(xc_offsets)
        ]

    def share_y(stat, into):
        return [send(stat.at[1], into.at[d - 1], ydev(d)) for d in range(1, 4)]

    def share_z(stat, into):
        return [send(stat.at[2], into.at[d - 1], zdev(d)) for d in range(1, 8)]

    def merged(copies, stat, level, into):
        arrive(copies)
        return merge(stat[level], [into[k] for k in range(len(copies))])

    sst_1s = share_xc(sstat, sst_1)
    lax.fori_loop(1, 8, emb_part, 0)
    emb[...] = acc[...].astype(BF16).reshape(2, 256, 1024)
    emb_cs = [send(emb.at[oc], emb_c, dev(c=oc))]
    sstat[1] = merged(sst_1s, sstat, 0, sst_1)
    sst_2s = share_y(sstat, sst_2)

    arrive(head_z)
    packs_z = send_pack(rep_offsets[:4])

    for p in range(4):
        values = tlog[p] + teacher(1, p)
        tlog[p] = values
        top = jnp.max(values, axis=0, keepdims=True)
        tstat[0, p : p + 1, :] = top
        tstat[0, 4 + p : 5 + p, :] = jnp.sum(jnp.exp(values - top), axis=0, keepdims=True)
    tst_1s = share_xc(tstat, tst_1)
    for p in range(4):
        values = tlog[p]
        top = tstat[0, p : p + 1, :]
        cstat[0, p : p + 1, :] = top
        cstat[0, 4 + p : 5 + p, :] = jnp.sum(
            jnp.exp(values - top) * (values - slog[p]), axis=0, keepdims=True
        )
    sstat[2] = merged(sst_2s, sstat, 1, sst_2)
    sst_3s = share_z(sstat, sst_3)
    tstat[1] = merged(tst_1s, tstat, 0, tst_1)
    tst_2s = share_y(tstat, tst_2)
    arrive(emb_cs)
    emb[c] = (emb[c].astype(F32) + emb_c[...].astype(F32)).astype(BF16)
    emb_ys = [
        send(emb.at[c, rows(((y + d) % 4) * 64, 64, 64)], emb_y.at[d - 1], ydev(d))
        for d in range(1, 4)
    ]
    tstat[2] = merged(tst_2s, tstat, 1, tst_2)
    tst_3s = share_z(tstat, tst_3)
    student_total = merged(sst_3s, sstat, 2, sst_3)
    student_lse = student_total[0:4] + jnp.log(student_total[4:8])
    mask = jnp.concatenate([meta[i // 2, i % 2, 3:4, :] for i in range(8)], axis=0)
    to_slot = position(lax.broadcasted_iota(jnp.int32, (128, 128), 1)) == lax.broadcasted_iota(
        jnp.int32, (128, 128), 0
    )
    mask = dot_nn(mask.astype(F32).astype(BF16), to_slot.astype(BF16))
    mask = jnp.concatenate(
        [jnp.concatenate([mask[2 * p : 2 * p + 1], mask[2 * p + 1 : 2 * p + 2]], axis=1) for p in range(4)],
        axis=0,
    )
    mask_total = jnp.sum(mask, axis=(0, 1), keepdims=True)
    sstat[3, 0:4, :] = student_lse
    sstat[3, 4:8, :] = mask * (8 * 128) / mask_total

    total = merged(tst_3s, tstat, 2, tst_3)
    teacher_lse = total[0:4] + jnp.log(total[4:8])
    tstat[3, 0:4, :] = teacher_lse
    tstat[3, 4:8, :] = total[4:8]

    def gradient(p):
        row = pl.ds(p, 1)
        student_prob = jnp.exp(slog[p] - sstat[3, row, :])
        teacher_prob = jnp.exp(tlog[p] - tstat[3, row, :])
        return (sstat[3, pl.ds(4 + p, 1), :] * (student_prob - teacher_prob)).astype(BF16)

    g_x = []
    for d in range(1, 4):
        p = (x + d) % 4
        gbuf[p] = gradient(p)
        g_x.append(send(gbuf.at[p], gx.at[x], xdev(d)))
    own_grad = gradient(x)
    gbuf[x] = own_grad
    gx[x] = own_grad
    cst_1s = share_xc(cstat, cst_1)

    arrive(emb_ys)
    mine = emb[c, rows(y * 64, 64, 64)].astype(F32)
    for d in range(3):
        mine = mine + emb_y[d].astype(F32)
    emb_2[...] = mine.astype(BF16)
    emb_zs = [
        send(emb_2.at[rows(((zl + d) % 4) * 16, 16, 16)], emb_z.at[d - 1], dev(zl=(zl + d) % 4))
        for d in range(1, 4)
    ]

    def hidden_part(k, half, first):
        tokens = gx[k, :, half * 128 : half * 128 + 128]
        product = dot_tn(tokens, tab[k * 2 + zh]).reshape(2, 64, 1024)
        if first:
            hp[half] = product
        else:
            hp[half] += product

    hp_cs = []
    for d in range(4):
        if d > 0:
            arrive([g_x[d - 1]])
        for half in range(2):
            hidden_part((x + 4 - d) % 4, half, d == 0)
            if d == 3:
                hp_cs.append(send(hp.at[half, oc], hp_c.at[half], dev(c=oc)))
    cstat[1] = merged(cst_1s, cstat, 0, cst_1)
    cst_2s = share_y(cstat, cst_2)

    def table_part(p, carry):
        part = dot_nn(gbuf[p], hid[p].reshape(256, 1024))

        @pl.when(p == 0)
        def _():
            base[...] = part

        @pl.when(p != 0)
        def _():
            base[...] += part

        return carry

    lax.fori_loop(0, 4, table_part, 0)
    h1_ys = []
    for half in range(2):
        arrive([hp_cs[half]])
        h1[half] = (hp[half, c] + hp_c[half]).reshape(4, 16, 1024)
        h1_ys.append(
            [
                send(h1.at[half, (y + d) % 4], h1_y.at[d - 1, half], ydev(d))
                for d in range(1, 4)
            ]
        )

    cstat[2] = merged(cst_2s, cstat, 1, cst_2)
    cst_3s = share_z(cstat, cst_3)
    for half in range(2):
        arrive(h1_ys[half])
        mine = h1[half, y]
        for d in range(3):
            mine = mine + h1_y[d, half]
        for i in range(4):
            h2[half, i] = mine[4 * i : 4 * i + 4]
    h2_zs = []
    for d in range(1, 8):
        to = (z + d) % 8
        h2_zs.append(send(h2.at[to // 4, to % 4], h2_z.at[d - 1], zdev(d)))
    arrive(emb_zs)
    mine = emb_2[rows(zl * 16, 16, 16)].astype(F32)
    for d in range(3):
        mine = mine + emb_z[d].astype(F32)
    mine = (mine * 32.0).astype(BF16)
    src_out[0] = mine[0:8]
    tgt_out[0] = mine[8:12]

    arrive(packs_x)
    arrive(packs_z)
    cross = merged(cst_3s, cstat, 2, cst_3)
    token_kl = cross[4:8] / tstat[3, 4:8, :] - tstat[3, 0:4, :] + sstat[3, 0:4, :]
    weight = sstat[3, 4:8, :]
    kl = jnp.sum(weight * token_kl, axis=(0, 1), keepdims=True) / (8 * 128)
    kl_out[...] = kl
    fullest = [meta[i // 2, i % 2, 6:7, 0:1] for i in range(8)]
    full_out[...] = functools.reduce(jnp.maximum, fullest)
    arrive(h2_zs)
    result = h2[zh, zl]
    for d in range(7):
        result = result + h2_z[d]
    hg_out[0] = result
    for copy in pending:
        copy.wait_send()


def add_packed(base, packs, meta, out):
    r = lax.axis_index("rep")
    owned = jnp.concatenate([meta[i // 2, i % 2, 5:6, :] for i in range(8)], axis=0) + 1
    sub_128 = lax.broadcasted_iota(jnp.int32, (128, 128), 0)
    lane_128 = lax.broadcasted_iota(jnp.int32, (128, 128), 1)
    own_slots = (sub_128 == r * PACK + lane_128 % PACK).astype(F32).astype(BF16)
    owned = dot_nn((owned & 255).astype(F32).astype(BF16), own_slots) + 256.0 * dot_nn(
        (owned >> 8).astype(F32).astype(BF16), own_slots
    )
    owned = jnp.where(sub_128[0:8] == lane_128[0:8] // PACK, owned, 0.0)
    owned = jnp.sum(owned, axis=0, keepdims=True).astype(jnp.int32) - 1
    spread = (owned == lax.broadcasted_iota(jnp.int32, (512, 128), 0)).astype(BF16)
    terms = packs[...].reshape(128, 1024)
    coarse = terms.astype(BF16)
    fine = (terms - coarse.astype(F32)).astype(BF16)
    lookup = dot_nn(spread, coarse) + dot_nn(spread, fine)
    out[...] = (base[...] + lookup * 32.0).astype(BF16)


def add_dense(base, src_cot, tgt_cot, meta, out, cots, total, lsem, ssem, rsem):
    v, r = lax.axis_index("vocab"), lax.axis_index("rep")
    copies = [
        pltpu.make_async_copy(src_cot.at[0], cots.at[r, pl.ds(0, 256)], lsem.at[0]),
        pltpu.make_async_copy(tgt_cot.at[0], cots.at[r, pl.ds(256, 128)], lsem.at[1]),
    ]
    for copy in copies:
        copy.start()
    barrier = pltpu.get_barrier_semaphore()
    peers = [(v, (r + d) % 8) for d in range(1, 8)]
    for peer in peers:
        pl.semaphore_signal(barrier, inc=1, device_id=peer, device_id_type=MESH)
    pl.semaphore_wait(barrier, 7)
    for copy in copies:
        copy.wait()
    sends = []
    for k, peer in enumerate(peers):
        sends.append(
            pltpu.make_async_remote_copy(
                src_ref=cots.at[r], dst_ref=cots.at[r], send_sem=ssem.at[k], recv_sem=rsem.at[k],
                device_id=peer, device_id_type=MESH,
            )
        )
        sends[-1].start()
    for copy in sends:
        copy.wait()
    total[...] = base[...]
    row = lax.broadcasted_iota(jnp.int32, (512, 128), 0) + (v * 4096 + r * 512)

    def one(i, carry):
        ids = meta[i // 2, i % 2]
        onehot = jnp.concatenate(
            [(ids[k : k + 1, :] == row).astype(BF16) for k in range(3)], axis=1
        )
        total[...] += dot_nn(onehot, cots[i]) * 32.0
        return carry

    lax.fori_loop(0, 8, one, 0)
    out[...] = total[...].astype(BF16)


def hand_over(*refs):
    half = len(refs) // 2
    for src, dst in zip(refs[:half], refs[half:]):
        dst[...] = src[...]


def on_device(
    src_ids, tgt_ids, tgt_mask, tgt_order, table, student_hidden, teacher_hidden, teacher_head,
    src_embed_grad, tgt_embed_grad,
):
    vmem = pl.BlockSpec(memory_space=pltpu.VMEM)
    hbm = pl.BlockSpec(memory_space=pl.ANY)

    def scratch(shape, dtype=BF16):
        return pltpu.VMEM(shape, dtype)

    def stats():
        return [
            scratch((4, 8, 256), F32), scratch((7, 8, 256), F32), scratch((3, 8, 256), F32),
            scratch((7, 8, 256), F32),
        ]

    outs = (
        jax.ShapeDtypeStruct((1, 8, 1024), BF16),
        jax.ShapeDtypeStruct((1, 4, 1024), BF16),
        jax.ShapeDtypeStruct((1, 1), F32),
        jax.ShapeDtypeStruct((1, 4, 1024), F32),
    )
    table_out = jax.ShapeDtypeStruct((512, 1024), BF16)
    results = pl.pallas_call(
        kernel,
        name="distill",
        out_shape=outs
        + (
            jax.ShapeDtypeStruct((1, 1), jnp.int32),
            jax.ShapeDtypeStruct((512, 1024), F32),
            jax.ShapeDtypeStruct((8, PACK, 1024), F32),
            jax.ShapeDtypeStruct((4, 2, 8, 128), jnp.int32),
        ),
        in_specs=[hbm, hbm, hbm, hbm, hbm, vmem, vmem, vmem, vmem, vmem],
        out_specs=(vmem,) * 8,
        scratch_shapes=[
            scratch((8, 512, 1024)),
            scratch((2, 512, 1024)),
            scratch((128, 1024)),
            scratch((4, 2, 128, 1024)),
            scratch((384, 1024)),
            scratch((8, PACK, 1024), F32),
            scratch((2, 4, 2, 512, 256)),
            scratch((2, 16, 256), F32),
            scratch((512, 128), jnp.int32),
            scratch((8, 512), jnp.int32),
            scratch((2, 4, 2, 128, 1024)),
            scratch((4, 512, 256), F32),
            scratch((4, 512, 256), F32),
            scratch((512, 1024), F32),
            scratch((4, 512, 256)),
            scratch((4, 512, 256)),
            scratch((2, 256, 1024)),
            scratch((64, 1024)),
            scratch((256, 1024)),
            scratch((3, 64, 1024)),
            scratch((3, 16, 1024)),
            *stats(),
            *stats(),
            *stats(),
            scratch((2, 2, 64, 1024), F32),
            scratch((2, 64, 1024), F32),
            scratch((2, 4, 16, 1024), F32),
            scratch((3, 2, 16, 1024), F32),
            scratch((2, 4, 4, 1024), F32),
            scratch((7, 4, 1024), F32),
            pltpu.SemaphoreType.DMA((16,)),
            pltpu.SemaphoreType.DMA((144,)),
            pltpu.SemaphoreType.DMA((144,)),
        ],
        compiler_params=pltpu.CompilerParams(
            collective_id=0, has_side_effects=True, vmem_limit_bytes=60 * 2**20
        ),
        cost_estimate=pl.CostEstimate(
            flops=12 * 10**9, bytes_accessed=16 * 2**20, transcendentals=2 * 10**6
        ),
    )(
        teacher_head, table, student_hidden, src_embed_grad, tgt_embed_grad, teacher_hidden,
        src_ids, tgt_ids, tgt_mask, tgt_order,
    )
    *results, fullest, base, packs, meta = results

    def packed_path(base, packs, meta):
        return pl.pallas_call(
            add_packed, name="add_packed", out_shape=table_out, in_specs=[vmem] * 3, out_specs=vmem,
        )(base, packs, meta)

    def dense_path(base, packs, meta):
        return pl.pallas_call(
            add_dense,
            name="add_dense",
            out_shape=table_out,
            in_specs=[vmem, hbm, hbm, vmem],
            out_specs=vmem,
            scratch_shapes=[
                scratch((8, 384, 1024)),
                scratch((512, 1024), F32),
                pltpu.SemaphoreType.DMA((2,)),
                pltpu.SemaphoreType.DMA((7,)),
                pltpu.SemaphoreType.DMA((7,)),
            ],
            compiler_params=pltpu.CompilerParams(
                collective_id=1, has_side_effects=True, vmem_limit_bytes=40 * 2**20
            ),
        )(base, src_embed_grad, tgt_embed_grad, meta)

    table_grad = lax.cond(fullest[0, 0] < PACK, packed_path, dense_path, base, packs, meta)
    src, tgt, kl, hidden_grad = pl.pallas_call(
        hand_over, name="hand_over", out_shape=outs, in_specs=[vmem] * 4, out_specs=(vmem,) * 4
    )(*results)
    return (src, tgt, kl[0, 0], hidden_grad, table_grad)


def solution(mesh):
    return jax.shard_map(
        on_device,
        mesh=mesh,
        in_specs=(
            P("rep", None),
            P("rep", None),
            P("rep", None),
            P("rep", None),
            P("vocab", None),
            P("rep", None, None),
            P("rep", "vocab", None),
            P("vocab", "rep"),
            P("rep", None, None),
            P("rep", None, None),
        ),
        out_specs=(
            P("rep", "vocab", None),
            P("rep", "vocab", None),
            P(),
            P("rep", "vocab", None),
            P(("vocab", "rep"), None),
        ),
        check_vma=False,
    )
```

```python
import functools

import jax
import jax.numpy as jnp
from jax import lax
from jax.experimental import pallas as pl
from jax.experimental.pallas import tpu as pltpu
from jax.sharding import PartitionSpec as P

MESH = pl.DeviceIdType.MESH
PACK = 16
NX, NY, NZL, NZH, NC = 4, 4, 4, 2, 2
NZ = NZL * NZH
F32, BF16 = jnp.float32, jnp.bfloat16


def dot_nt(a, b):
    return lax.dot_general(a, b, (((1,), (1,)), ((), ())), preferred_element_type=F32)


def dot_nn(a, b):
    return lax.dot_general(a, b, (((1,), (0,)), ((), ())), preferred_element_type=F32)


def dot_tn(a, b):
    return lax.dot_general(a, b, (((0,), (0,)), ((), ())), preferred_element_type=F32)


def merge(own, others):
    groups = own.shape[0] // 4
    tops = [piece[0:4] for piece in [own] + others]
    top = functools.reduce(jnp.maximum, tops)
    total = [0.0] * (groups - 1)
    for piece, piece_top in zip([own] + others, tops):
        factor = jnp.exp(piece_top - top)
        for g in range(1, groups):
            total[g - 1] = total[g - 1] + piece[4 * g : 4 * g + 4] * factor
    return jnp.concatenate([top] + total, axis=0)


def kernel(
    head, table, hidden_in, src_cot, tgt_cot, states_in, src_ids, tgt_ids, tgt_mask, tgt_order,
    src_out, tgt_out, kl_out, hg_out, full_out, base, packs, meta,
    tab, headbuf, hid_raw, hid, cot, pack, st, st_f32, slot_ids, orders, order_st, slog, tlog,
    acc, gbuf, gx, emb, emb_2, emb_c, emb_y, emb_z,
    sstat, sst_1, sst_2, sst_3, tstat, tst_1, tst_2, tst_3, cstat, cst_1, cst_2, cst_3,
    hp, hp_c, h1, h1_y, h2, h2_z,
    lsem, ssem, rsem,
):
    v, r = lax.axis_index("vocab"), lax.axis_index("rep")
    y, zl, c = v // 8, (v // 2) % 4, v % 2
    x, zh = r // 2, r % 2
    z = zh * 4 + zl
    oc = 1 - c
    oz = 1 - zh

    def dev(y=y, zl=zl, c=c, x=x, zh=zh):
        return ((y * 4 + zl) * 2 + c, x * 2 + zh)

    def zdev(d):
        to = (z + d) % 8
        return dev(zl=to % 4, zh=to // 4)

    def xdev(d):
        return dev(x=(x + d) % 4)

    def ydev(d):
        return dev(y=(y + d) % 4)

    def xcdev(dx, dc):
        return dev(x=(x + dx) % 4, c=(c + dc) % 2)

    used = {"l": 0, "r": 0}
    pending = []

    def local(src, dst):
        i = used["l"]
        used["l"] += 1
        copy = pltpu.make_async_copy(src, dst, lsem.at[i])
        copy.start()
        return copy

    def send(src, dst, to):
        i = used["r"]
        used["r"] += 1
        copy = pltpu.make_async_remote_copy(
            src_ref=src, dst_ref=dst, send_sem=ssem.at[i], recv_sem=rsem.at[i],
            device_id=to, device_id_type=MESH,
        )
        copy.start()
        pending.append(copy)
        return copy

    def same(ref, to):
        return send(ref, ref, to)

    def arrive(copies):
        for copy in copies:
            copy.wait_recv()

    barrier = pltpu.get_barrier_semaphore()
    rep_offsets = [(dx, dz) for dz in (1, 0) for dx in range(4) if (dx, dz) != (0, 0)]
    xc_offsets = [(dx, dc) for dc in (0, 1) for dx in range(4) if (dx, dc) != (0, 0)]
    peers = [dev(x=(x + dx) % 4, zh=(zh + dz) % 2) for dx, dz in rep_offsets]
    peers += [zdev(d) for d in range(1, 8) if d != 4]
    peers += [ydev(d) for d in range(1, 4)]
    peers += [xcdev(dx, 1) for dx in range(4)]
    for peer in peers:
        pl.semaphore_signal(barrier, inc=1, device_id=peer, device_id_type=MESH)

    def rows(start, step, count):
        return pl.ds(pl.multiple_of(start, step), count)

    x_cols = rows(x * 256, 256, 256)
    own_raw = local(hidden_in.at[0], hid_raw)
    own_head = local(head.at[rows(r * 512, 512, 512)], headbuf.at[0, :, x_cols])
    own_cot = [
        local(src_cot.at[0], cot.at[pl.ds(0, 256)]),
        local(tgt_cot.at[0], cot.at[pl.ds(256, 128)]),
    ]
    tab_copies = [local(table.at[pl.ds(b * 512, 512)], tab.at[b]) for b in range(8)]

    st_8th = rows(c * 256 + y * 64 + zl * 16, 16, 16)
    st_y = rows(c * 256 + y * 64, 64, 64)
    st_c = rows(c * 256, 256, 256)
    for k in range(8):
        st_f32[k // 4, (k % 4) * 4 : (k % 4) * 4 + 4, :] = states_in[
            0, :, k * 256 : (k + 1) * 256
        ].astype(F32)
    for half in range(2):
        st[half, x, zh, st_8th, :] = st_f32[half].astype(BF16)
    own_slot = c * 64 + y * 16 + lax.broadcasted_iota(jnp.int32, (16, 128), 0)

    def position(s):
        return (s // 16) % 4 * 32 + (s // 4) % 4 * 8 + s // 64 * 4 + s % 4

    pick = (position(own_slot) == lax.broadcasted_iota(jnp.int32, (16, 128), 1)).astype(BF16)
    hid_8th = rows(c * 64 + y * 16, 16, 16)
    hid_half = rows(c * 64, 64, 64)
    own_raw.wait()
    hid[x, zh, hid_8th, :] = dot_nn(pick, hid_raw[...]).astype(BF16)

    pl.semaphore_wait(barrier, len(peers))

    st_zs = [same(st.at[:, x, zh, st_8th, :], zdev(d)) for d in range(1, 8)]
    hid_z = [same(hid.at[x, zh, hid_8th], dev(zh=oz))]

    def send_head(offsets):
        copies = []
        for dx, dz in offsets:
            to_x, to_zh = (x + dx) % 4, (zh + dz) % 2
            block = head.at[rows((to_x * 2 + to_zh) * 512, 512, 512)]
            copies.append(send(block, headbuf.at[dz, :, x_cols], dev(x=to_x, zh=to_zh)))
        return copies


    def st_y_of(d):
        return rows(c * 256 + (y + 4 - d) % 4 * 64, 64, 64)

    def hid_8th_of(d):
        return rows(c * 64 + (y + 4 - d) % 4 * 16, 16, 16)

    arrive(st_zs)
    st_ya = [same(st.at[0, x, :, st_y, :], ydev(d)) for d in range(1, 4)]
    st_xb = [same(st.at[1, x, :, st_y, :], xdev(d)) for d in range(1, 4)]
    arrive(hid_z)
    hid_x = [same(hid.at[x, :, hid_8th, :], xdev(d)) for d in range(1, 4)]
    arrive(st_ya)
    st_xa = [same(st.at[0, x, :, st_c, :], xdev(d)) for d in range(1, 4)]
    arrive(st_xb)
    st_yb = [same(st.at[1, :, :, st_y, :], ydev(d)) for d in range(1, 4)]
    head_z = send_head(rep_offsets[:4])
    head_x = send_head(rep_offsets[4:])
    to_core = [
        same(st.at[0, x, :, st_c, :], dev(c=oc)),
        same(st.at[1, :, :, st_y, :], dev(c=oc)),
    ]
    ids = jnp.concatenate([src_ids[...], tgt_ids[...]], axis=1)
    pieces = jnp.concatenate(
        [ids & 255, (ids >> 8) & 255, ids >> 16, jnp.zeros((13, 384), jnp.int32)], axis=0
    ).astype(F32).astype(BF16)
    s = lax.broadcasted_iota(jnp.int32, (384, 512), 1)
    source = lax.broadcasted_iota(jnp.int32, (384, 512), 0)
    e = s % 16
    chip = (s // 64) % 4 * 8 + (s // 16) % 4 * 2 + s // 256
    wanted = jnp.where(e < 8, chip * 8 + e, 256 + chip * 4 + e - 8)
    moved = dot_nn(pieces, ((wanted == source) & (e < 12)).astype(BF16))
    power = lax.broadcasted_iota(jnp.int32, (16, 128), 0)
    power = jnp.where(power == 0, 1, jnp.where(power == 1, 256, jnp.where(power == 2, 65536, 0)))
    power = power.astype(F32).astype(BF16)
    slot_id = dot_tn(moved.astype(BF16), power).astype(jnp.int32) - v * 4096
    empty = lax.broadcasted_iota(jnp.int32, (512, 128), 0) % 16 >= 12
    slot_ids[...] = jnp.where(empty, -1, slot_id)

    id_col = dot_tn(pieces, power).astype(jnp.int32)[:, 0:1]
    later = lax.broadcasted_iota(jnp.int32, (384, 384), 0) < lax.broadcasted_iota(
        jnp.int32, (384, 384), 1
    )
    repeat = jnp.max(
        jnp.where((id_col == ids) & later, 1, 0), axis=0, keepdims=True
    )
    ahead = ((id_col >> 9) == (ids >> 9)) & (ids < id_col) & (repeat == 0)
    place_col = jnp.sum(jnp.where(ahead, 1, 0), axis=1, keepdims=True)
    target = lax.broadcasted_iota(jnp.int32, (384, 128), 1)
    chosen = ((id_col >> 9) == v * 8 + target // PACK) & (place_col == target % PACK)
    row_lane = jnp.max(jnp.where(chosen, id_col & 511, -1), axis=0, keepdims=True)
    for copy in own_cot:
        copy.wait()
    pack[...] = dot_tn(chosen.astype(F32).astype(BF16), cot[...]).reshape(8, PACK, 1024)
    packs[r] = pack[r]
    fullest = jnp.max(place_col, axis=(0, 1), keepdims=True)
    meta[x, zh] = jnp.concatenate(
        [
            src_ids[:, 0:128], src_ids[:, 128:256], tgt_ids[...], tgt_mask[...], tgt_order[...],
            row_lane, jnp.broadcast_to(fullest, (1, 128)), jnp.zeros((1, 128), jnp.int32),
        ],
        axis=0,
    )
    meta_r = [
        same(meta.at[x, zh], dev(x=(x + dx) % 4, zh=(zh + dz) % 2)) for dx, dz in rep_offsets
    ]

    def send_pack(offsets):
        copies = []
        for dx, dz in offsets:
            to_x, to_zh = (x + dx) % 4, (zh + dz) % 2
            copies.append(send(pack.at[to_x * 2 + to_zh], packs.at[r], dev(x=to_x, zh=to_zh)))
        return copies

    packs_x = send_pack(rep_offsets[4:])

    row_lane_512 = lax.broadcasted_iota(jnp.int32, (512, 512), 1)

    def emb_part(b, carry):
        onehot = (slot_ids[:, 0:1] - b * 512 == row_lane_512).astype(BF16)
        part = dot_nn(onehot, tab[b])

        @pl.when(b == 0)
        def _():
            acc[...] = part

        @pl.when(b != 0)
        def _():
            acc[...] += part

        return carry

    for copy in tab_copies:
        copy.wait()
    lax.fori_loop(0, 1, emb_part, 0)
    arrive(hid_x)
    hid_y = [same(hid.at[:, :, hid_8th, :], ydev(d)) for d in range(1, 4)]
    hid_c = [same(hid.at[:, :, hid_8th, :], dev(c=oc))]
    for k, d in enumerate((1, 3, 2)):
        arrive([st_xa[d - 1]])
        to_core.append(same(st.at[0, (x + 4 - d) % 4, :, st_c, :], dev(c=oc)))
        arrive([st_yb[d - 1]])
        to_core.append(same(st.at[1, :, :, st_y_of(d), :], dev(c=oc)))
    for d in (1, 3, 2):
        arrive([hid_y[d - 1]])
        hid_c.append(same(hid.at[:, :, hid_8th_of(d), :], dev(c=oc)))

    k_lane = lax.broadcasted_iota(jnp.int32, (128, 512), 1)
    arrival = (k_lane // 64) % 4 * 32 + (k_lane // 16) % 4 * 8 + k_lane // 256 * 4 + k_lane % 4
    expand = (lax.broadcasted_iota(jnp.int32, (128, 512), 0) == arrival).astype(BF16)
    arrive(meta_r)
    order = jnp.concatenate([meta[i // 2, i % 2, 4:5, :] for i in range(8)], axis=0)
    order = (order // 4) % 2 * 64 + (order // 32) * 16 + (order // 8) % 4 * 4 + order % 4
    orders[...] = dot_nn(order.astype(F32).astype(BF16), expand).astype(jnp.int32)
    slot = lax.broadcasted_iota(jnp.int32, (128, 512), 0)
    part = lax.broadcasted_iota(jnp.int32, (128, 512), 1) // 4 % 4
    arrive(to_core)

    def place(i, carry):
        px, pz = i // 2, i % 2
        order = orders[pl.ds(i, 1), :]
        hit = jnp.where(order == slot, part, -1)
        move = jnp.concatenate([(hit == j).astype(BF16) for j in range(4)], axis=0)
        for half in range(2):
            placed = dot_nn(move, st[half, px, pz]).astype(BF16)
            for j in range(4):
                block = half * 4 + j
                order_st[
                    (zh + block) % 2, px, pz, :, block // 2 * 256 : block // 2 * 256 + 256
                ] = placed[j * 128 : (j + 1) * 128]
        return carry

    lax.fori_loop(0, 8, place, 0)

    def teacher(half, p):
        return dot_nt(headbuf[half], order_st[half, p].reshape(256, 1024))

    def teacher_near(p, carry):
        tlog[p] = teacher(0, p)
        return carry

    own_head.wait()
    arrive(head_x)
    lax.fori_loop(0, 4, teacher_near, 0)

    arrive(hid_c)
    own_rows = tab.at[r]

    def student(p, carry):
        slog[p] = dot_nt(own_rows[...], hid[p].reshape(256, 1024))
        return carry

    lax.fori_loop(0, 4, student, 0)
    for p in range(4):
        values = slog[p]
        top = jnp.max(values, axis=0, keepdims=True)
        sstat[0, p : p + 1, :] = top
        sstat[0, 4 + p : 5 + p, :] = jnp.sum(jnp.exp(values - top), axis=0, keepdims=True)

    def share_xc(stat, into):
        return [
            send(stat.at[0], into.at[k], xcdev(dx, dc)) for k, (dx, dc) in enumerate(xc_offsets)
        ]

    def share_y(stat, into):
        return [send(stat.at[1], into.at[d - 1], ydev(d)) for d in range(1, 4)]

    def share_z(stat, into):
        return [send(stat.at[2], into.at[d - 1], zdev(d)) for d in range(1, 8)]

    def merged(copies, stat, level, into):
        arrive(copies)
        return merge(stat[level], [into[k] for k in range(len(copies))])

    sst_1s = share_xc(sstat, sst_1)
    lax.fori_loop(1, 8, emb_part, 0)
    emb[...] = acc[...].astype(BF16).reshape(2, 256, 1024)
    emb_cs = [send(emb.at[oc], emb_c, dev(c=oc))]
    sstat[1] = merged(sst_1s, sstat, 0, sst_1)
    sst_2s = share_y(sstat, sst_2)

    arrive(head_z)
    packs_z = send_pack(rep_offsets[:4])

    for p in range(4):
        values = tlog[p] + teacher(1, p)
        tlog[p] = values
        top = jnp.max(values, axis=0, keepdims=True)
        tstat[0, p : p + 1, :] = top
        tstat[0, 4 + p : 5 + p, :] = jnp.sum(jnp.exp(values - top), axis=0, keepdims=True)
    tst_1s = share_xc(tstat, tst_1)
    for p in range(4):
        values = tlog[p]
        top = tstat[0, p : p + 1, :]
        cstat[0, p : p + 1, :] = top
        cstat[0, 4 + p : 5 + p, :] = jnp.sum(
            jnp.exp(values - top) * (values - slog[p]), axis=0, keepdims=True
        )
    sstat[2] = merged(sst_2s, sstat, 1, sst_2)
    sst_3s = share_z(sstat, sst_3)
    tstat[1] = merged(tst_1s, tstat, 0, tst_1)
    tst_2s = share_y(tstat, tst_2)
    arrive(emb_cs)
    emb[c] = (emb[c].astype(F32) + emb_c[...].astype(F32)).astype(BF16)
    emb_ys = [
        send(emb.at[c, rows(((y + d) % 4) * 64, 64, 64)], emb_y.at[d - 1], ydev(d))
        for d in range(1, 4)
    ]
    tstat[2] = merged(tst_2s, tstat, 1, tst_2)
    tst_3s = share_z(tstat, tst_3)
    student_total = merged(sst_3s, sstat, 2, sst_3)
    student_lse = student_total[0:4] + jnp.log(student_total[4:8])
    mask = jnp.concatenate([meta[i // 2, i % 2, 3:4, :] for i in range(8)], axis=0)
    to_slot = position(lax.broadcasted_iota(jnp.int32, (128, 128), 1)) == lax.broadcasted_iota(
        jnp.int32, (128, 128), 0
    )
    mask = dot_nn(mask.astype(F32).astype(BF16), to_slot.astype(BF16))
    mask = jnp.concatenate(
        [jnp.concatenate([mask[2 * p : 2 * p + 1], mask[2 * p + 1 : 2 * p + 2]], axis=1) for p in range(4)],
        axis=0,
    )
    mask_total = jnp.sum(mask, axis=(0, 1), keepdims=True)
    sstat[3, 0:4, :] = student_lse
    sstat[3, 4:8, :] = mask * (8 * 128) / mask_total

    total = merged(tst_3s, tstat, 2, tst_3)
    teacher_lse = total[0:4] + jnp.log(total[4:8])
    tstat[3, 0:4, :] = teacher_lse
    tstat[3, 4:8, :] = total[4:8]

    def gradient(p):
        row = pl.ds(p, 1)
        student_prob = jnp.exp(slog[p] - sstat[3, row, :])
        teacher_prob = jnp.exp(tlog[p] - tstat[3, row, :])
        return (sstat[3, pl.ds(4 + p, 1), :] * (student_prob - teacher_prob)).astype(BF16)

    g_x = []
    for d in range(1, 4):
        p = (x + d) % 4
        gbuf[p] = gradient(p)
        g_x.append(send(gbuf.at[p], gx.at[x], xdev(d)))
    own_grad = gradient(x)
    gbuf[x] = own_grad
    gx[x] = own_grad
    cst_1s = share_xc(cstat, cst_1)

    arrive(emb_ys)
    mine = emb[c, rows(y * 64, 64, 64)].astype(F32)
    for d in range(3):
        mine = mine + emb_y[d].astype(F32)
    emb_2[...] = mine.astype(BF16)
    emb_zs = [
        send(emb_2.at[rows(((zl + d) % 4) * 16, 16, 16)], emb_z.at[d - 1], dev(zl=(zl + d) % 4))
        for d in range(1, 4)
    ]

    def hidden_part(k, half, first):
        tokens = gx[k, :, half * 128 : half * 128 + 128]
        product = dot_tn(tokens, tab[k * 2 + zh]).reshape(2, 64, 1024)
        if first:
            hp[half] = product
        else:
            hp[half] += product

    hp_cs = []
    for d in range(4):
        if d > 0:
            arrive([g_x[d - 1]])
        for half in range(2):
            hidden_part((x + 4 - d) % 4, half, d == 0)
            if d == 3:
                hp_cs.append(send(hp.at[half, oc], hp_c.at[half], dev(c=oc)))
    cstat[1] = merged(cst_1s, cstat, 0, cst_1)
    cst_2s = share_y(cstat, cst_2)

    def table_part(p, carry):
        part = dot_nn(gbuf[p], hid[p].reshape(256, 1024))

        @pl.when(p == 0)
        def _():
            base[...] = part

        @pl.when(p != 0)
        def _():
            base[...] += part

        return carry

    lax.fori_loop(0, 4, table_part, 0)
    h1_ys = []
    for half in range(2):
        arrive([hp_cs[half]])
        h1[half] = (hp[half, c] + hp_c[half]).reshape(4, 16, 1024)
        h1_ys.append(
            [
                send(h1.at[half, (y + d) % 4], h1_y.at[d - 1, half], ydev(d))
                for d in range(1, 4)
            ]
        )

    cstat[2] = merged(cst_2s, cstat, 1, cst_2)
    cst_3s = share_z(cstat, cst_3)
    for half in range(2):
        arrive(h1_ys[half])
        mine = h1[half, y]
        for d in range(3):
            mine = mine + h1_y[d, half]
        for i in range(4):
            h2[half, i] = mine[4 * i : 4 * i + 4]
    h2_zs = []
    for d in range(1, 8):
        to = (z + d) % 8
        h2_zs.append(send(h2.at[to // 4, to % 4], h2_z.at[d - 1], zdev(d)))
    arrive(emb_zs)
    mine = emb_2[rows(zl * 16, 16, 16)].astype(F32)
    for d in range(3):
        mine = mine + emb_z[d].astype(F32)
    mine = (mine * 32.0).astype(BF16)
    src_out[0] = mine[0:8]
    tgt_out[0] = mine[8:12]

    arrive(packs_x)
    arrive(packs_z)
    cross = merged(cst_3s, cstat, 2, cst_3)
    token_kl = cross[4:8] / tstat[3, 4:8, :] - tstat[3, 0:4, :] + sstat[3, 0:4, :]
    weight = sstat[3, 4:8, :]
    kl = jnp.sum(weight * token_kl, axis=(0, 1), keepdims=True) / (8 * 128)
    kl_out[...] = kl
    fullest = [meta[i // 2, i % 2, 6:7, 0:1] for i in range(8)]
    full_out[...] = functools.reduce(jnp.maximum, fullest)
    arrive(h2_zs)
    result = h2[zh, zl]
    for d in range(7):
        result = result + h2_z[d]
    hg_out[0] = result
    for copy in pending:
        copy.wait_send()


def add_packed(base, packs, meta, out):
    r = lax.axis_index("rep")
    owned = jnp.concatenate([meta[i // 2, i % 2, 5:6, :] for i in range(8)], axis=0) + 1
    sub_128 = lax.broadcasted_iota(jnp.int32, (128, 128), 0)
    lane_128 = lax.broadcasted_iota(jnp.int32, (128, 128), 1)
    own_slots = (sub_128 == r * PACK + lane_128 % PACK).astype(F32).astype(BF16)
    owned = dot_nn((owned & 255).astype(F32).astype(BF16), own_slots) + 256.0 * dot_nn(
        (owned >> 8).astype(F32).astype(BF16), own_slots
    )
    owned = jnp.where(sub_128[0:8] == lane_128[0:8] // PACK, owned, 0.0)
    owned = jnp.sum(owned, axis=0, keepdims=True).astype(jnp.int32) - 1
    spread = (owned == lax.broadcasted_iota(jnp.int32, (512, 128), 0)).astype(BF16)
    terms = packs[...].reshape(128, 1024)
    coarse = terms.astype(BF16)
    fine = (terms - coarse.astype(F32)).astype(BF16)
    lookup = dot_nn(spread, coarse) + dot_nn(spread, fine)
    out[...] = (base[...] + lookup * 32.0).astype(BF16)


def add_dense(base, src_cot, tgt_cot, meta, out, cots, total, lsem, ssem, rsem):
    v, r = lax.axis_index("vocab"), lax.axis_index("rep")
    copies = [
        pltpu.make_async_copy(src_cot.at[0], cots.at[r, pl.ds(0, 256)], lsem.at[0]),
        pltpu.make_async_copy(tgt_cot.at[0], cots.at[r, pl.ds(256, 128)], lsem.at[1]),
    ]
    for copy in copies:
        copy.start()
    barrier = pltpu.get_barrier_semaphore()
    peers = [(v, (r + d) % 8) for d in range(1, 8)]
    for peer in peers:
        pl.semaphore_signal(barrier, inc=1, device_id=peer, device_id_type=MESH)
    pl.semaphore_wait(barrier, 7)
    for copy in copies:
        copy.wait()
    sends = []
    for k, peer in enumerate(peers):
        sends.append(
            pltpu.make_async_remote_copy(
                src_ref=cots.at[r], dst_ref=cots.at[r], send_sem=ssem.at[k], recv_sem=rsem.at[k],
                device_id=peer, device_id_type=MESH,
            )
        )
        sends[-1].start()
    for copy in sends:
        copy.wait()
    total[...] = base[...]
    row = lax.broadcasted_iota(jnp.int32, (512, 128), 0) + (v * 4096 + r * 512)

    def one(i, carry):
        ids = meta[i // 2, i % 2]
        onehot = jnp.concatenate(
            [(ids[k : k + 1, :] == row).astype(BF16) for k in range(3)], axis=1
        )
        total[...] += dot_nn(onehot, cots[i]) * 32.0
        return carry

    lax.fori_loop(0, 8, one, 0)
    out[...] = total[...].astype(BF16)


def hand_over(*refs):
    half = len(refs) // 2
    for src, dst in zip(refs[:half], refs[half:]):
        dst[...] = src[...]


def on_device(
    src_ids, tgt_ids, tgt_mask, tgt_order, table, student_hidden, teacher_hidden, teacher_head,
    src_embed_grad, tgt_embed_grad,
):
    vmem = pl.BlockSpec(memory_space=pltpu.VMEM)
    hbm = pl.BlockSpec(memory_space=pl.ANY)

    def scratch(shape, dtype=BF16):
        return pltpu.VMEM(shape, dtype)

    def stats():
        return [
            scratch((4, 8, 256), F32), scratch((7, 8, 256), F32), scratch((3, 8, 256), F32),
            scratch((7, 8, 256), F32),
        ]

    outs = (
        jax.ShapeDtypeStruct((1, 8, 1024), BF16),
        jax.ShapeDtypeStruct((1, 4, 1024), BF16),
        jax.ShapeDtypeStruct((1, 1), F32),
        jax.ShapeDtypeStruct((1, 4, 1024), F32),
    )
    table_out = jax.ShapeDtypeStruct((512, 1024), BF16)
    results = pl.pallas_call(
        kernel,
        name="distill",
        out_shape=outs
        + (
            jax.ShapeDtypeStruct((1, 1), jnp.int32),
            jax.ShapeDtypeStruct((512, 1024), F32),
            jax.ShapeDtypeStruct((8, PACK, 1024), F32),
            jax.ShapeDtypeStruct((4, 2, 8, 128), jnp.int32),
        ),
        in_specs=[hbm, hbm, hbm, hbm, hbm, vmem, vmem, vmem, vmem, vmem],
        out_specs=(vmem,) * 8,
        scratch_shapes=[
            scratch((8, 512, 1024)),
            scratch((2, 512, 1024)),
            scratch((128, 1024)),
            scratch((4, 2, 128, 1024)),
            scratch((384, 1024)),
            scratch((8, PACK, 1024), F32),
            scratch((2, 4, 2, 512, 256)),
            scratch((2, 16, 256), F32),
            scratch((512, 128), jnp.int32),
            scratch((8, 512), jnp.int32),
            scratch((2, 4, 2, 128, 1024)),
            scratch((4, 512, 256), F32),
            scratch((4, 512, 256), F32),
            scratch((512, 1024), F32),
            scratch((4, 512, 256)),
            scratch((4, 512, 256)),
            scratch((2, 256, 1024)),
            scratch((64, 1024)),
            scratch((256, 1024)),
            scratch((3, 64, 1024)),
            scratch((3, 16, 1024)),
            *stats(),
            *stats(),
            *stats(),
            scratch((2, 2, 64, 1024), F32),
            scratch((2, 64, 1024), F32),
            scratch((2, 4, 16, 1024), F32),
            scratch((3, 2, 16, 1024), F32),
            scratch((2, 4, 4, 1024), F32),
            scratch((7, 4, 1024), F32),
            pltpu.SemaphoreType.DMA((16,)),
            pltpu.SemaphoreType.DMA((144,)),
            pltpu.SemaphoreType.DMA((144,)),
        ],
        compiler_params=pltpu.CompilerParams(
            collective_id=0, has_side_effects=True, vmem_limit_bytes=60 * 2**20
        ),
        cost_estimate=pl.CostEstimate(
            flops=12 * 10**9, bytes_accessed=16 * 2**20, transcendentals=2 * 10**6
        ),
    )(
        teacher_head, table, student_hidden, src_embed_grad, tgt_embed_grad, teacher_hidden,
        src_ids, tgt_ids, tgt_mask, tgt_order,
    )
    *results, fullest, base, packs, meta = results

    def packed_path(base, packs, meta):
        return pl.pallas_call(
            add_packed, name="add_packed", out_shape=table_out, in_specs=[vmem] * 3, out_specs=vmem,
        )(base, packs, meta)

    def dense_path(base, packs, meta):
        return pl.pallas_call(
            add_dense,
            name="add_dense",
            out_shape=table_out,
            in_specs=[vmem, hbm, hbm, vmem],
            out_specs=vmem,
            scratch_shapes=[
                scratch((8, 384, 1024)),
                scratch((512, 1024), F32),
                pltpu.SemaphoreType.DMA((2,)),
                pltpu.SemaphoreType.DMA((7,)),
                pltpu.SemaphoreType.DMA((7,)),
            ],
            compiler_params=pltpu.CompilerParams(
                collective_id=1, has_side_effects=True, vmem_limit_bytes=40 * 2**20
            ),
        )(base, src_embed_grad, tgt_embed_grad, meta)

    table_grad = lax.cond(fullest[0, 0] < PACK, packed_path, dense_path, base, packs, meta)
    src, tgt, kl, hidden_grad = pl.pallas_call(
        hand_over, name="hand_over", out_shape=outs, in_specs=[vmem] * 4, out_specs=(vmem,) * 4
    )(*results)
    return (src, tgt, kl[0, 0], hidden_grad, table_grad)


def solution(mesh):
    return jax.shard_map(
        on_device,
        mesh=mesh,
        in_specs=(
            P("rep", None),
            P("rep", None),
            P("rep", None),
            P("rep", None),
            P("vocab", None),
            P("rep", None, None),
            P("rep", "vocab", None),
            P("vocab", "rep"),
            P("rep", None, None),
            P("rep", None, None),
        ),
        out_specs=(
            P("rep", "vocab", None),
            P("rep", "vocab", None),
            P(),
            P("rep", "vocab", None),
            P(("vocab", "rep"), None),
        ),
        check_vma=False,
    )
```
